128 devices in a mesh: seq: 32 (over x, y, core), head: 4 (over z).
Axes of the slice: x: 4, y: 4, z: 4, core: 2. Of those that a mesh axis runs over, the one named last changes fastest.
Arguments:
- x_in: bfloat16 [24576, 16384], P('seq', 'head'), may hold values from -6 to 6
- z_in: bfloat16 [24576, 16384], P('seq', 'head'), may hold values from -6 to 6
- bc_in: bfloat16 [24576, 2, 2048], P('seq', None, 'head'), may hold values from -6 to 6
- dt_in: float32 [24576, 256], P('seq', 'head'), may hold values from -6 to 6
- conv_x_weight: float32 [4, 16384], P(None, 'head'), may hold values from -3 to 3
- conv_x_bias: float32 [16384], P('head'), may hold values from -0.5 to 0.5
- conv_bc_weight: float32 [4, 2, 2048], P(None, None, 'head'), may hold values from -3 to 3
- conv_bc_bias: float32 [2, 2048], P(None, 'head'), may hold values from -0.5 to 0.5
- dt_bias: float32 [256], P('head'), may hold values from -1 to 1
- a_log: float32 [256], P('head')
- norm_gain: float32 [16384], P('head'), may hold values from 0.5 to 1.5
- reward_w: float32 [16384], P('head'), may hold values from -0.046875 to 0.046875
- step_ends: int32 [64], replicated, may hold values from 0 to 24575, as said below
Outputs:
- normed: bfloat16 [24576, 16384], P('seq', 'head')
- rewards: float32 [64], replicated
The draws below stay inside these ranges and needn't reach their ends.
Inputs may be any that keep to these rules, and one draw needn't show every extreme that they name: `step_ends`: each is a token position of the trace; the last step ends at the trace's last token.
All inputs are finite; a program needn't handle non-finite values.
Results may differ from the reference program's by a relative error of at most 0.0034.
Values may be sent and summed in bfloat16 or wider, within the bound.
No kernel may reach another device: no remote copies, remote signals or barrier semaphores. Data moves between devices by JAX's collectives and lax.ppermute only.
A program may use at most 448 MiB of HBM per device.

```python
import jax
import jax.numpy as jnp
from jax import lax

HEADS = 256
HEAD_DIM = 64
STATE = 256
GROUPS = 8
CONV = 4
D_INNER = 16384
SPAN = 256
STEPS = 64
TOKENS = 24576


def draw_a_log(key, part):
    key = jax.random.fold_in(key, 11)
    first, second, third = jax.random.split(key, 3)
    share = 0.5
    quick = jax.random.uniform(first, (HEADS,)) < share
    slow_rate = jnp.exp(jax.random.uniform(second, (HEADS,), minval=jnp.log(0.3), maxval=jnp.log(2.0))) / TOKENS
    fast_rate = jnp.exp(jax.random.uniform(third, (HEADS,), minval=jnp.log(0.03), maxval=jnp.log(0.12)))
    return jnp.log(jnp.where(quick, fast_rate, slow_rate)).astype(jnp.float32)


def draw_step_ends(key, part):
    key = jax.random.fold_in(key, 12)
    places = jax.random.randint(key, (STEPS,), 0, TOKENS)
    return places.at[STEPS - 1].set(TOKENS - 1).astype(jnp.int32)


def levels(key, shape, cuts, smallest, high):
    def one(axis_at, blocks):
        heights = jax.random.uniform(jax.random.fold_in(jax.random.fold_in(key, 6), axis_at), (blocks,), jnp.float32, smallest / len(cuts), high / len(cuts))
        return jnp.repeat(jnp.exp(heights), shape[axis_at] // blocks).reshape((-1,) + (1,) * (len(shape) - axis_at - 1))

    loudness = one(*cuts[0])
    for cut in cuts[1:]:
        loudness = loudness * one(*cut)
    return loudness


def gaussian(key, extent, deviation, most, cuts=(), held_as=jnp.bfloat16):
    values = deviation * jax.random.normal(key, extent, jnp.float32)
    if cuts:
        values = values * levels(key, extent, cuts, -0.22, 0.18)
    return jnp.clip(values, -most, most).astype(held_as)


def setup_inputs(seed: int = 0) -> dict:
    key_of = jax.random.split(jax.random.key(seed), 14)
    return {
        "x_in": gaussian(key_of[0], (TOKENS, D_INNER), 1.0, 6.0, ((0, 32), (1, 4))),
        "z_in": gaussian(key_of[1], (TOKENS, D_INNER), 1.0, 6.0, ((0, 32), (1, 4))),
        "bc_in": gaussian(key_of[2], (TOKENS, 2, GROUPS * STATE), 1.0, 6.0, ((0, 32), (2, 4))),
        "dt_in": gaussian(key_of[3], (TOKENS, HEADS), 1.0, 6.0, ((0, 32), (1, 4)), jnp.float32),
        "conv_x_weight": gaussian(key_of[4], (CONV, D_INNER), CONV ** -0.5, 3.0, ((1, 4),), jnp.float32),
        "conv_x_bias": jnp.clip(jax.random.uniform(key_of[5], (D_INNER,), jnp.float32, -0.5, 0.5) * levels(key_of[5], (D_INNER,), ((0, 4),), -0.4, 0.0), -0.5, 0.5),
        "conv_bc_weight": gaussian(key_of[6], (CONV, 2, GROUPS * STATE), CONV ** -0.5, 3.0, ((2, 4),), jnp.float32),
        "conv_bc_bias": jnp.clip(jax.random.uniform(key_of[7], (2, GROUPS * STATE), jnp.float32, -0.5, 0.5) * levels(key_of[7], (2, GROUPS * STATE), ((1, 4),), -0.4, 0.0), -0.5, 0.5),
        "dt_bias": jnp.clip(jax.random.uniform(key_of[8], (HEADS,), jnp.float32, -1.0, 1.0) * levels(key_of[8], (HEADS,), ((0, 4),), -0.4, 0.0), -1.0, 1.0),
        "a_log": draw_a_log(jax.random.fold_in(key_of[13], 71), 0),
        "norm_gain": jnp.clip(1.0 + 0.1 * jax.random.normal(key_of[10], (D_INNER,), jnp.float32), 0.5, 1.5),
        "reward_w": gaussian(key_of[11], (D_INNER,), D_INNER ** -0.5, 0.046875, ((0, 4),), jnp.float32),
        "step_ends": draw_step_ends(jax.random.fold_in(key_of[13], 71), 0),
    }


def conv_silu(series, taps, offset):
    length = series.shape[0]
    width = taps.shape[0]
    padded = jnp.concatenate([jnp.zeros((width - 1,) + series.shape[1:], series.dtype), series], 0)
    total = jnp.zeros(series.shape, jnp.float32) + offset
    for tap in range(width):
        total = total + taps[tap] * padded[tap:tap + length].astype(jnp.float32)
    return jax.nn.silu(total).astype(jnp.bfloat16)

def span_terms(state, x_blk, b_blk, c_blk, dt_blk, log_blk):
    length = x_blk.shape[0]
    row_idx = lax.broadcasted_iota(jnp.int32, (length, length), 0)
    col_idx = lax.broadcasted_iota(jnp.int32, (length, length), 1)
    lower = row_idx >= col_idx
    running = jnp.cumsum(log_blk, axis=0)
    along = jnp.transpose(running, (1, 2, 0))
    spread = along[..., :, None] - along[..., None, :]
    decay = jnp.where(lower, jnp.exp(jnp.where(lower, spread, 0.0)), 0.0) * jnp.transpose(dt_blk, (1, 2, 0))[..., None, :]
    scores = jnp.einsum('tgn,sgn->gts', c_blk.astype(jnp.float32), b_blk.astype(jnp.float32))
    mixing = (scores[:, None] * decay).astype(jnp.bfloat16)
    inner = jnp.einsum('ghts,sghp->tghp', mixing.astype(jnp.float32), x_blk.astype(jnp.float32))
    carried = jnp.exp(running)[..., None] * jnp.einsum('tgn,ghnp->tghp', c_blk.astype(jnp.float32), state, precision=lax.Precision.HIGHEST)
    weights = jnp.exp(running[-1][None] - running) * dt_blk
    scaled = (b_blk.astype(jnp.float32)[:, :, None, :] * weights[..., None]).astype(jnp.bfloat16)
    update = jnp.einsum('sghn,sghp->ghnp', scaled.astype(jnp.float32), x_blk.astype(jnp.float32))
    state = jnp.exp(running[-1])[..., None, None] * state + update
    return (state, inner + carried, running)

def gated_norm(values, gate, gain):
    length = values.shape[0]
    groups_here = values.shape[1]
    grouped = values.reshape(length, groups_here, -1)
    gated = grouped * jax.nn.silu(gate.reshape(length, groups_here, -1).astype(jnp.float32))
    meansq = lax.optimization_barrier(jnp.mean(gated * gated, axis=-1, keepdims=True))
    result = gated * lax.rsqrt(meansq + 1e-05) * gain.reshape(groups_here, -1)
    return result.reshape(length, -1).astype(jnp.bfloat16)

def reference(x_in, z_in, bc_in, dt_in, conv_x_weight, conv_x_bias, conv_bc_weight, conv_bc_bias, dt_bias, a_log, norm_gain, reward_w, step_ends):
    conv_x = conv_silu(x_in, conv_x_weight, conv_x_bias)
    conv_bc = conv_silu(bc_in, conv_bc_weight, conv_bc_bias)
    per_group = HEADS // GROUPS
    count = TOKENS // SPAN
    step_size = jax.nn.softplus(dt_in + dt_bias)
    log_decay = step_size * -jnp.exp(a_log)
    blocks = (conv_x.reshape(count, SPAN, GROUPS, per_group, HEAD_DIM), conv_bc[:, 0].reshape(count, SPAN, GROUPS, STATE), conv_bc[:, 1].reshape(count, SPAN, GROUPS, STATE), step_size.reshape(count, SPAN, GROUPS, per_group), log_decay.reshape(count, SPAN, GROUPS, per_group), z_in.reshape(count, SPAN, D_INNER))

    def advance(state, items):
        x_blk, b_blk, c_blk, dt_blk, log_blk, z_blk = items
        state, values, running = span_terms(state, x_blk, b_blk, c_blk, dt_blk, log_blk)
        return (state, gated_norm(values, z_blk, norm_gain))
    start = jnp.zeros((GROUPS, per_group, STATE, HEAD_DIM), jnp.float32)
    _, normed = lax.scan(advance, start, blocks)
    normed = normed.reshape(TOKENS, D_INNER)
    picked = normed[step_ends].astype(jnp.float32)
    rewards = lax.optimization_barrier(jnp.sum(picked * reward_w, axis=-1))
    return (normed, rewards)
```

```python
import functools

import jax
import jax.numpy as jnp
import numpy as np
from jax import lax
from jax.experimental import pallas as pl
from jax.experimental.pallas import tpu as pltpu
from jax.sharding import PartitionSpec as P

HEAD_DIM = 64
STATE = 256
PER_GROUP = 32
LANES = PER_GROUP * HEAD_DIM
CHUNK = 128
TAIL = 16
EXTRA = 16
TILE = 512
LOG2E = 1.4426950408889634
F32 = jnp.float32
BF16 = jnp.bfloat16
VMEM_LIMIT = 56 * 1024 * 1024


def params(*semantics):
    return pltpu.CompilerParams(
        dimension_semantics=semantics or None, vmem_limit_bytes=VMEM_LIMIT
    )


def dot(a, b, ca=1, cb=0):
    return lax.dot_general(a, b, (((ca,), (cb,)), ((), ())), preferred_element_type=F32)


def split2(v):
    high = v.astype(BF16)
    return high, (v - high.astype(F32)).astype(BF16)


def split3(v):
    high = v.astype(BF16)
    rest = v - high.astype(F32)
    mid = rest.astype(BF16)
    return high, mid, (rest - mid.astype(F32)).astype(BF16)


def silu(v):
    half = 0.5 * v
    return half + half * jnp.tanh(half)


def decay_kernel(dt_ref, ld_ref, row_ref, col_ref, ehl_ref, whl_ref, eabs_ref, wabs_ref, tot_ref):
    heads, rows = dt_ref.shape
    count = rows // CHUNK
    u = lax.broadcasted_iota(jnp.int32, (CHUNK, CHUNK), 0)
    t = lax.broadcasted_iota(jnp.int32, (CHUNK, CHUNK), 1)
    upto = (u <= t).astype(BF16)
    after = (u > t).astype(BF16)
    running, suffix, total = [], [], []
    for c in range(count):
        ld = ld_ref[:, c * CHUNK : (c + 1) * CHUNK]
        terms = jnp.concatenate(split3(ld), axis=0)
        r = dot(terms, upto)
        s = dot(terms, after)
        r = r[:heads] + r[heads : 2 * heads] + r[2 * heads :]
        s = s[:heads] + s[heads : 2 * heads] + s[2 * heads :]
        running.append(r)
        suffix.append(s)
        total.append(r[:, CHUNK - 1 :])
    before = [jnp.zeros_like(total[0])]
    for c in range(count):
        before.append(before[-1] + total[c])
    behind = [jnp.zeros_like(total[0])]
    for c in range(count - 1, 0, -1):
        behind.append(behind[-1] + total[c])
    behind = behind[::-1]

    def put(ref, v, c):
        for g in range(heads // PER_GROUP):
            part = v[g * PER_GROUP : (g + 1) * PER_GROUP]
            high, low = split2(part)
            ref[g, 0:PER_GROUP, c * CHUNK : (c + 1) * CHUNK] = high
            ref[g, PER_GROUP : 2 * PER_GROUP, c * CHUNK : (c + 1) * CHUNK] = low

    for c in range(count):
        where = slice(c * CHUNK, (c + 1) * CHUNK)
        dt = dt_ref[:, where]
        row_ref[:, where] = running[c] - jnp.log2(dt)
        col = running[c].T
        for g in range(heads // PER_GROUP):
            col_ref[g, where, :] = col[:, g * PER_GROUP : (g + 1) * PER_GROUP]
        put(ehl_ref, jnp.exp2(running[c]), c)
        put(whl_ref, jnp.exp2(suffix[c]) * dt, c)
        put(eabs_ref, jnp.exp2(running[c] + before[c]), c)
        put(wabs_ref, jnp.exp2(suffix[c] + behind[c]) * dt, c)
    tot_ref[...] = before[count] + jnp.zeros((heads, 128), F32)


def decays(dt, ld):
    heads, rows = dt.shape
    groups = heads // PER_GROUP
    pair = jax.ShapeDtypeStruct((groups, 2 * PER_GROUP, rows), BF16)
    return pl.pallas_call(
        decay_kernel,
        out_shape=[
            jax.ShapeDtypeStruct((heads, rows), F32),
            jax.ShapeDtypeStruct((groups, rows, PER_GROUP), F32),
            pair,
            pair,
            pair,
            pair,
            jax.ShapeDtypeStruct((heads, 128), F32),
        ],
        compiler_params=params(),
    )(dt, ld)


def conv_column(pad, series, tail, taps, offset, store):
    rows = series.shape[0]
    pad[0:8, :] = tail[TAIL - 8 :, :].astype(F32)
    pad[8 : 8 + rows, :] = series[...].astype(F32)
    for start in range(0, rows, CHUNK):
        total = offset[...] + taps[3:4, :] * pad[8 + start : 8 + start + CHUNK, :]
        for k in range(3):
            total = total + taps[k : k + 1, :] * pad[5 + k + start : 5 + k + start + CHUNK, :]
        store(start, silu(total))


def state_kernel(
    x_ref, xt_ref, b_ref, bt_ref, c_ref, ct_ref, wx_ref, ox_ref, wb_ref, ob_ref, wc_ref, oc_ref,
    wabs_ref, spread_ref, tot_ref,
    cx_ref, cb_ref, cc_ref, state_ref, pad, scaled, bturn,
):
    rows = x_ref.shape[0]

    @pl.when(pl.program_id(0) == 0)
    def _():
        for src, tail, taps, offset, dst in (
            (b_ref, bt_ref, wb_ref, ob_ref, cb_ref),
            (c_ref, ct_ref, wc_ref, oc_ref, cc_ref),
        ):
            for lane in range(0, STATE, 128):
                cut = (slice(None), slice(lane, lane + 128))

                def store(start, v, dst=dst, lane=lane):
                    dst[start : start + CHUNK, lane : lane + 128] = v.astype(BF16)

                conv_column(pad, src.at[cut], tail.at[cut], taps.at[cut], offset.at[cut], store)
        bturn[...] = cb_ref[...].T

    spread = spread_ref[...]
    weight = wabs_ref[0]
    for lane in range(0, TILE, 128):
        cut = (slice(None), slice(lane, lane + 128))

        def store(start, v, lane=lane):
            v = v.astype(BF16)
            cx_ref[start : start + CHUNK, lane : lane + 128] = v
            w = dot(weight[:, start : start + CHUNK], spread[:, lane : lane + 128], 0, 0)
            scaled[start : start + CHUNK, lane : lane + 128] = (w * v.astype(F32)).astype(BF16)

        conv_column(pad, x_ref.at[cut], xt_ref.at[cut], wx_ref.at[cut], ox_ref.at[cut], store)
    state_ref[0:STATE, :] = dot(bturn[...], scaled[...]).astype(BF16)
    state_ref[STATE:, :] = dot(tot_ref[0], spread[:PER_GROUP]).astype(BF16)


def local_states(g, x, x_tail, bc, bc_tail, wx, ox, wbc, obc, wabs, spread, tot):
    rows = x.shape[0]
    groups = x.shape[1] // LANES
    tiles = LANES // TILE
    lane = lambda j: (0, g * tiles + j)
    at = lambda n: lambda j: (0, n)
    part = lambda n, w: [
        pl.BlockSpec((rows, STATE), at(n)),
        pl.BlockSpec((TAIL, STATE), at(n)),
    ]
    return pl.pallas_call(
        state_kernel,
        grid=(tiles,),
        in_specs=[
            pl.BlockSpec((rows, TILE), lane),
            pl.BlockSpec((TAIL, TILE), lane),
            *part(g, STATE),
            *part(groups + g, STATE),
            pl.BlockSpec((4, TILE), lane),
            pl.BlockSpec((1, TILE), lane),
            pl.BlockSpec((4, STATE), at(g)),
            pl.BlockSpec((1, STATE), at(g)),
            pl.BlockSpec((4, STATE), at(groups + g)),
            pl.BlockSpec((1, STATE), at(groups + g)),
            pl.BlockSpec((1, 2 * PER_GROUP, rows), lambda j: (g, 0, 0)),
            pl.BlockSpec((2 * PER_GROUP, TILE), lambda j: (0, j)),
            pl.BlockSpec((1, EXTRA, PER_GROUP), lambda j: (g, 0, 0)),
        ],
        out_specs=[
            pl.BlockSpec((rows, TILE), lambda j: (0, j)),
            pl.BlockSpec((rows, STATE), lambda j: (0, 0)),
            pl.BlockSpec((rows, STATE), lambda j: (0, 0)),
            pl.BlockSpec((STATE + EXTRA, TILE), lambda j: (0, j)),
        ],
        out_shape=[
            jax.ShapeDtypeStruct((rows, LANES), BF16),
            jax.ShapeDtypeStruct((rows, STATE), BF16),
            jax.ShapeDtypeStruct((rows, STATE), BF16),
            jax.ShapeDtypeStruct((STATE + EXTRA, LANES), BF16),
        ],
        scratch_shapes=[
            pltpu.VMEM((rows + 8, 128), F32),
            pltpu.VMEM((rows, TILE), BF16),
            pltpu.VMEM((STATE, rows), BF16),
        ],
        compiler_params=params("arbitrary"),
        cost_estimate=pl.CostEstimate(
            flops=2 * rows * STATE * LANES, bytes_accessed=4 * rows * LANES, transcendentals=rows * LANES
        ),
    )(x, x_tail, bc, bc_tail, bc, bc_tail, wx, ox, wbc, obc, wbc, obc, wabs, spread, tot)


def values_kernel(
    x_ref, b_ref, c_ref, row_ref, col_ref, ehl_ref, whl_ref, spread_ref, out_ref, state, state16
):
    chunk = pl.program_id(0)

    @pl.when(chunk == 0)
    def _():
        state[...] = jnp.zeros_like(state)
        state16[...] = jnp.zeros_like(state16)

    b = b_ref[...]
    c = c_ref[...]
    scores = dot(c, b, 1, 1)
    t = lax.broadcasted_iota(jnp.int32, (CHUNK, CHUNK), 0)
    s = lax.broadcasted_iota(jnp.int32, (CHUNK, CHUNK), 1)
    scores = jnp.where(t >= s, scores, 0.0)
    bturn = b.T
    left = lax.broadcasted_iota(jnp.int32, (CHUNK, 128), 1) < HEAD_DIM
    decay = ehl_ref[0]
    weight = whl_ref[0]
    for lane in range(0, LANES, 256):
        cut = slice(lane, lane + 256)
        spread = spread_ref[:, cut]
        grown = dot(decay, spread, 0, 0)
        carried = grown * dot(c, state16[:, cut])
        for pair in range(2):
            first = lane // HEAD_DIM + 2 * pair
            at = slice(lane + 128 * pair, lane + 128 * pair + 128)
            mixes = []
            for h in (first, first + 1):
                spread_log = col_ref[0, :, h : h + 1] - row_ref[h : h + 1, :]
                mixes.append((scores * jnp.exp2(jnp.minimum(spread_log, 64.0))).astype(BF16))
            both = dot(jnp.concatenate(mixes, axis=0), x_ref[:, at])
            inner = jnp.where(left, both[:CHUNK], both[CHUNK:])
            out_ref[:, at] = (inner + carried[:, 128 * pair : 128 * pair + 128]).astype(out_ref.dtype)
        x = x_ref[:, cut].astype(F32)
        scaled = (dot(weight, spread, 0, 0) * x).astype(BF16)
        later = grown[CHUNK - 1 :, :] * state[:, cut] + dot(bturn, scaled)
        state[:, cut] = later
        state16[:, cut] = later.astype(BF16)


def local_values(g, x, b, c, row, col, ehl, whl, spread):
    rows = x.shape[0]
    return pl.pallas_call(
        values_kernel,
        grid=(rows // CHUNK,),
        in_specs=[
            pl.BlockSpec((CHUNK, LANES), lambda i: (i, 0)),
            pl.BlockSpec((CHUNK, STATE), lambda i: (i, 0)),
            pl.BlockSpec((CHUNK, STATE), lambda i: (i, 0)),
            pl.BlockSpec((PER_GROUP, CHUNK), lambda i: (g, i)),
            pl.BlockSpec((1, CHUNK, PER_GROUP), lambda i: (g, i, 0)),
            pl.BlockSpec((1, 2 * PER_GROUP, CHUNK), lambda i: (g, 0, i)),
            pl.BlockSpec((1, 2 * PER_GROUP, CHUNK), lambda i: (g, 0, i)),
            pl.BlockSpec((2 * PER_GROUP, LANES), lambda i: (0, 0)),
        ],
        out_specs=pl.BlockSpec((CHUNK, LANES), lambda i: (i, 0)),
        out_shape=jax.ShapeDtypeStruct((rows, LANES), F32),
        scratch_shapes=[pltpu.VMEM((STATE, LANES), F32), pltpu.VMEM((STATE, LANES), BF16)],
        compiler_params=params("arbitrary"),
        cost_estimate=pl.CostEstimate(
            flops=8 * rows * STATE * LANES, bytes_accessed=8 * rows * LANES, transcendentals=rows * CHUNK * PER_GROUP
        ),
    )(x, b, c, row, col, ehl, whl, spread)


def norm_kernel(values_ref, c_ref, state_ref, eabs_ref, spread_ref, z_ref, gain_ref, *rest):
    out_ref, gated = rest[-2:]
    rows = values_ref.shape[0]
    c = c_ref[...]
    decay = eabs_ref[0]
    squares = jnp.zeros((rows, 128), F32)
    for lane in range(0, LANES, 256):
        cut = slice(lane, lane + 256)
        v = values_ref[:, cut].astype(F32) + dot(decay, spread_ref[:, cut], 0, 0) * dot(c, state_ref[:, cut])
        v = v * silu(z_ref[:, cut].astype(F32))
        gated[:, cut] = v
        squares = squares + v[:, :128] * v[:, :128] + v[:, 128:] * v[:, 128:]
    scale = lax.rsqrt(jnp.sum(squares, axis=1, keepdims=True) * (1.0 / LANES) + 1e-05)
    for lane in range(0, LANES, 256):
        cut = slice(lane, lane + 256)
        out_ref[:, cut] = (gated[:, cut] * scale * gain_ref[:, cut]).astype(BF16)


def gated_norm(g, values, c, state, eabs, spread, z, gain, target):
    rows = values.shape[0]
    return pl.pallas_call(
        norm_kernel,
        grid=(rows // CHUNK,),
        in_specs=[
            pl.BlockSpec((CHUNK, LANES), lambda i: (i, 0)),
            pl.BlockSpec((CHUNK, STATE), lambda i: (i, 0)),
            pl.BlockSpec((STATE, LANES), lambda i: (0, 0)),
            pl.BlockSpec((1, 2 * PER_GROUP, CHUNK), lambda i: (g, 0, i)),
            pl.BlockSpec((2 * PER_GROUP, LANES), lambda i: (0, 0)),
            pl.BlockSpec((CHUNK, LANES), lambda i: (i, g)),
            pl.BlockSpec((1, LANES), lambda i: (0, g)),
        ]
        + ([] if target is None else [pl.BlockSpec(memory_space=pl.ANY)]),
        out_specs=pl.BlockSpec((CHUNK, LANES), lambda i: (i, g)),
        out_shape=jax.ShapeDtypeStruct(z.shape, BF16),
        scratch_shapes=[pltpu.VMEM((CHUNK, LANES), F32)],
        input_output_aliases={} if target is None else {7: 0},
        compiler_params=params("arbitrary"),
        cost_estimate=pl.CostEstimate(
            flops=2 * rows * STATE * LANES, bytes_accessed=8 * rows * LANES, transcendentals=rows * LANES
        ),
    )(values, c, state, eabs, spread, z, gain, *(() if target is None else (target,)))


def total_of(payload):
    extra = payload[STATE : STATE + 3].astype(F32)
    return extra[0:1] + extra[1:2] + extra[2:3]


def with_total(state, total):
    rows = jnp.concatenate(split3(total), axis=0)
    rows = jnp.pad(rows, ((0, EXTRA - 3), (0, 0)))
    return jnp.concatenate([state.astype(BF16), rows], axis=0)


def advance(state, payload):
    return jnp.exp2(total_of(payload)) * state + payload[:STATE].astype(F32)


def over(value, move):
    count = lax.axis_size("seq")
    return lax.ppermute(value, "seq", [(i, move(i)) for i in range(count) if move(i) is not None])


def entering_state(payload):
    place = lax.axis_index("seq")
    core, y = place % 2, place // 2 % 4
    half = LANES // 2
    quarter = half // 4
    halves = lambda n: lax.dynamic_slice_in_dim(payload, n * half, half, 1)
    mine, other = halves(core), over(halves(1 - core), lambda i: i ^ 1)
    first = jnp.where(core == 0, mine, other)
    second = jnp.where(core == 0, other, mine)
    chip = with_total(
        advance(first[:STATE].astype(F32), second), total_of(first) + total_of(second)
    )
    along_y = lambda k: lambda i: i // 8 * 8 + (i // 2 + k) % 4 * 2 + i % 2
    piece = lambda n: lax.dynamic_slice_in_dim(chip, n * quarter, quarter, 1)
    came = jnp.stack([piece(y)] + [over(piece((y + k) % 4), along_y(k)) for k in (1, 2, 3)])
    parts = [lax.dynamic_index_in_dim(came, (y - n) % 4, 0, False) for n in range(4)]
    state, total = parts[0][:STATE].astype(F32), total_of(parts[0])
    for n in range(1, 4):
        state, total = advance(state, parts[n]), total + total_of(parts[n])
    row = with_total(state, total)
    near, mid, far = (
        over(row, lambda i, k=k: i + 8 * k if i + 8 * k < 32 else None) for k in (1, 2, 3)
    )
    state = advance(advance(far[:STATE].astype(F32), mid), near)
    entering = []
    for n in range(4):
        entering.append(state.astype(BF16))
        state = advance(state, parts[n])
    entering = jnp.stack(entering)
    give = lambda n: lax.dynamic_index_in_dim(entering, n, 0, False)
    back = jnp.stack([give(y)] + [over(give((y + k) % 4), along_y(k)) for k in (1, 2, 3)])
    chip_in = jnp.concatenate(
        [lax.dynamic_index_in_dim(back, (y - n) % 4, 0, False) for n in range(4)], axis=1
    )
    later = advance(chip_in.astype(F32), first).astype(BF16)
    keep = jnp.where(core == 0, chip_in, later)
    got = over(jnp.where(core == 0, later, chip_in), lambda i: i ^ 1)
    return jnp.concatenate([jnp.where(core == 0, keep, got), jnp.where(core == 0, got, keep)], axis=1)


def per_device(
    x_in, z_in, bc_in, dt_in, conv_x_weight, conv_x_bias, conv_bc_weight, conv_bc_bias,
    dt_bias, a_log, norm_gain, reward_w, step_ends,
):
    rows, channels = x_in.shape
    groups = channels // LANES
    bc = bc_in.reshape(rows, -1)
    following = lambda v: over(v, lambda i: i + 1 if i + 1 < 32 else None)
    x_tail = following(x_in[rows - TAIL :])
    bc_tail = following(bc_in[rows - TAIL :].reshape(TAIL, -1))
    dt = jax.nn.softplus(dt_in.T + dt_bias[:, None])
    ld = dt * (-LOG2E * jnp.exp(a_log))[:, None]
    row, col, ehl, whl, eabs, wabs, tot = decays(dt, ld)
    tot = jnp.stack(split3(tot[:, 0].reshape(groups, PER_GROUP)), axis=1)
    tot = jnp.pad(tot, ((0, 0), (0, EXTRA - 3), (0, 0)))
    head = np.arange(LANES) // HEAD_DIM
    spread = jnp.asarray(np.arange(2 * PER_GROUP)[:, None] % PER_GROUP == head, BF16)
    wx, ox = conv_x_weight, conv_x_bias[None]
    wbc, obc = conv_bc_weight.reshape(4, -1), conv_bc_bias.reshape(1, -1)
    made = [
        local_states(g, x_in, x_tail, bc, bc_tail, wx, ox, wbc, obc, wabs, spread, tot)
        for g in range(groups)
    ]
    states = [entering_state(m[3]) for m in made]
    values = [
        local_values(g, m[0], m[1], m[2], row, col, ehl, whl, spread) for g, m in enumerate(made)
    ]
    normed = None
    for g, m in enumerate(made):
        normed = gated_norm(g, values[g], m[2], states[g], eabs, spread, z_in, norm_gain[None], normed)
    local_pos = step_ends - lax.axis_index("seq") * rows
    inside = (local_pos >= 0) & (local_pos < rows)
    picked = jnp.take(normed, jnp.clip(local_pos, 0, rows - 1), axis=0).astype(F32)
    terms = jnp.where(inside, jnp.sum(picked * reward_w, axis=-1), 0.0)
    devices = lax.axis_size("seq") * lax.axis_size("head")
    terms = lax.all_to_all(jnp.broadcast_to(terms, (devices, terms.shape[0])), ("seq", "head"), 0, 0)
    return normed, jnp.sum(terms, axis=0)


def solution(mesh):
    return jax.shard_map(
        per_device,
        mesh=mesh,
        in_specs=(
            P("seq", "head"),
            P("seq", "head"),
            P("seq", None, "head"),
            P("seq", "head"),
            P(None, "head"),
            P("head"),
            P(None, None, "head"),
            P(None, "head"),
            P("head"),
            P("head"),
            P("head"),
            P("head"),
            P(),
        ),
        out_specs=(P("seq", "head"), P()),
        check_vma=False,
    )
```

```python
import functools

import jax
import jax.numpy as jnp
import numpy as np
from jax import lax
from jax.experimental import pallas as pl
from jax.experimental.pallas import tpu as pltpu
from jax.sharding import PartitionSpec as P

HEAD_DIM = 64
STATE = 256
PER_GROUP = 32
LANES = PER_GROUP * HEAD_DIM
CHUNK = 128
TAIL = 16
EXTRA = 16
TILE = 512
ROWS = 256
BLOCK = 2 * CHUNK
VTILE = 512
HALVES = 1
LOG2E = 1.4426950408889634
F32 = jnp.float32
BF16 = jnp.bfloat16
VMEM_LIMIT = 56 * 1024 * 1024


def params(*semantics):
    return pltpu.CompilerParams(
        dimension_semantics=semantics or None, vmem_limit_bytes=VMEM_LIMIT
    )


def dot(a, b, ca=1, cb=0):
    return lax.dot_general(a, b, (((ca,), (cb,)), ((), ())), preferred_element_type=F32)


def split2(v):
    high = v.astype(BF16)
    return high, (v - high.astype(F32)).astype(BF16)


def split3(v):
    high = v.astype(BF16)
    rest = v - high.astype(F32)
    mid = rest.astype(BF16)
    return high, mid, (rest - mid.astype(F32)).astype(BF16)


def silu(v):
    half = 0.5 * v
    return half + half * jnp.tanh(half)


def decay_kernel(
    dtin_ref, bias_ref, alog_ref, run_ref, row_ref, ehl_ref, whl_ref, eabs_ref, wabs_ref, tot_ref
):
    heads, rows = dtin_ref.shape
    count = rows // CHUNK
    h0 = lax.broadcasted_iota(jnp.int32, (heads, heads), 0)
    h1 = lax.broadcasted_iota(jnp.int32, (heads, heads), 1)
    upright = lambda v: jnp.sum(jnp.where(h0 == h1, v, 0.0), axis=1, keepdims=True)
    bias = upright(bias_ref[...])
    rate = upright(-LOG2E * jnp.exp(alog_ref[...]))
    u = lax.broadcasted_iota(jnp.int32, (CHUNK, CHUNK), 0)
    t = lax.broadcasted_iota(jnp.int32, (CHUNK, CHUNK), 1)
    upto = (u <= t).astype(BF16)
    after = (u > t).astype(BF16)
    steps, running, suffix, kept = [], [], [], []
    for c in range(count):
        v = dtin_ref[:, c * CHUNK : (c + 1) * CHUNK] + bias
        dt = jnp.maximum(v, 0.0) + jnp.log1p(jnp.exp(-jnp.abs(v)))
        terms = jnp.concatenate(split3(dt * rate), axis=0)
        r = dot(terms, upto)
        s = dot(terms, after)
        r = r[:heads] + r[heads : 2 * heads] + r[2 * heads :]
        s = s[:heads] + s[heads : 2 * heads] + s[2 * heads :]
        steps.append(dt)
        running.append(r)
        suffix.append(s)
    def put(ref, v, c):
        where = slice(c * CHUNK, (c + 1) * CHUNK)
        ref[where, 0:heads], ref[where, heads : 2 * heads] = split2(v)

    whole = jnp.zeros((1, heads), F32)
    for c in range(count):
        where = slice(c * CHUNK, (c + 1) * CHUNK)
        run_ref[:, where] = running[c]
        row_ref[:, where] = running[c] - jnp.log2(steps[c])
        run, rest, dt = running[c].T, suffix[c].T, steps[c].T
        grown, weight = jnp.exp2(run), jnp.exp2(rest) * dt
        put(ehl_ref, grown, c)
        put(whl_ref, weight, c)
        put(eabs_ref, grown * jnp.exp2(whole), c)
        whole = whole + run[CHUNK - 1 :, :]
        kept.append((weight, run[CHUNK - 1 :, :]))
    later = jnp.zeros((1, heads), F32)
    for c in range(count - 1, -1, -1):
        put(wabs_ref, kept[c][0] * jnp.exp2(later), c)
        later = later + kept[c][1]
    high, mid, low = split3(whole)
    place = lax.broadcasted_iota(jnp.int32, (EXTRA, heads), 0)
    terms = jnp.where(
        place == 0,
        high.astype(F32),
        jnp.where(place == 1, mid.astype(F32), jnp.where(place == 2, low.astype(F32), 0.0)),
    ).astype(BF16)
    tot_ref[:, 0:heads] = terms
    tot_ref[:, heads : 2 * heads] = jnp.zeros_like(terms)


def decays(dt_in, bias, a_log):
    heads, rows = dt_in.shape
    pair = jax.ShapeDtypeStruct((rows, 2 * heads), BF16)
    return pl.pallas_call(
        decay_kernel,
        out_shape=[
            jax.ShapeDtypeStruct((heads, rows), F32),
            jax.ShapeDtypeStruct((heads, rows), F32),
            pair,
            pair,
            pair,
            pair,
            jax.ShapeDtypeStruct((EXTRA, 2 * heads), BF16),
        ],
        compiler_params=params(),
        cost_estimate=pl.CostEstimate(flops=10**8, bytes_accessed=2 * 10**6, transcendentals=heads * rows * 5),
    )(dt_in, bias, a_log)


def conv_column(pad, series, tail, taps, offset, store):
    rows = series.shape[0]
    pad[0:8, :] = tail[...].astype(F32)[TAIL - 8 :]
    pad[8 : 8 + rows, :] = series[...].astype(F32)
    for start in range(0, rows, CHUNK):
        total = offset + taps[3] * pad[8 + start : 8 + start + CHUNK, :]
        for k in range(3):
            total = total + taps[k] * pad[5 + k + start : 5 + k + start + CHUNK, :]
        store(start, silu(total))


def state_kernel(core_ref, x_ref, xt_ref, wx_ref, ox_ref, wabs_ref, spread_ref, tot_ref, *rest):
    cx_ref, state_ref, pad, scaled, bturn = rest[-5:]
    if len(rest) == 6:
        made_ref = rest[0]

        @pl.when(pl.program_id(0) == 0)
        def _():
            bturn[...] = made_ref[...].T

    else:
        b_ref, bt_ref, c_ref, ct_ref, wb_ref, ob_ref, cb_ref, cc_ref = rest[:8]

        @pl.when(pl.program_id(0) == 0)
        def _():
            for n, (src, tail, dst) in enumerate(((b_ref, bt_ref, cb_ref), (c_ref, ct_ref, cc_ref))):
                for lane in range(0, STATE, 128):
                    cut = (slice(None), slice(lane, lane + 128))

                    def store(start, v, dst=dst, lane=lane):
                        dst[start : start + CHUNK, lane : lane + 128] = v.astype(BF16)

                    taps = [wb_ref[k, n : n + 1, lane : lane + 128] for k in range(4)]
                    offset = ob_ref[n : n + 1, lane : lane + 128]
                    conv_column(pad, src.at[cut], tail.at[cut], taps, offset, store)
            bturn[...] = cb_ref[...].T

    for lane in range(0, TILE, 128):
        own = slice(lane, lane + 128)
        cut = (slice(None), own)

        def store(start, v, own=own):
            v = v.astype(BF16)
            cx_ref[start : start + CHUNK, own] = v
            w = dot(wabs_ref[start : start + CHUNK, :], spread_ref[0, :, own])
            scaled[start : start + CHUNK, own] = (w * v.astype(F32)).astype(BF16)

        taps = [wx_ref[k : k + 1, own] for k in range(4)]
        conv_column(pad, x_ref.at[cut], xt_ref.at[cut], taps, ox_ref[:, own], store)
    state_ref[0:STATE, :] = dot(bturn[...], scaled[...]).astype(BF16)
    state_ref[STATE:, :] = dot(tot_ref[...], spread_ref[0]).astype(BF16)


def group_of(turn, core):
    return core[0] if turn else 1 - core[0]


def local_states(turn, half, core, x, tails, wx, ox, wabs, spread, tot, bc, wbc, obc, made=None):
    rows, channels = x.shape
    groups = channels // LANES
    width = LANES // HALVES
    tiles = width // TILE
    first = channels // STATE
    lane = lambda j, core: (0, (group_of(turn, core) * HALVES + half) * tiles + j)
    own = lambda shift: lambda j, core: (0, shift + group_of(turn, core))
    still = lambda j, core: (0, 0)
    out = lambda j, core: (0, j)
    if made is None:
        ends = [
            pl.BlockSpec((rows, STATE), own(0)),
            pl.BlockSpec((TAIL, STATE), own(first)),
            pl.BlockSpec((rows, STATE), own(groups)),
            pl.BlockSpec((TAIL, STATE), own(first + groups)),
            pl.BlockSpec((4, 2, STATE), lambda j, core: (0, 0, group_of(turn, core))),
            pl.BlockSpec((2, STATE), own(0)),
        ]
        last = (bc, tails, bc, tails, wbc, obc)
    else:
        ends = [pl.BlockSpec((rows, STATE), still)]
        last = (made,)
    fresh = 2 if made is None else 0
    return pl.pallas_call(
        state_kernel,
        grid_spec=pltpu.PrefetchScalarGridSpec(
            num_scalar_prefetch=1,
            grid=(tiles,),
            in_specs=[
                pl.BlockSpec((rows, TILE), lane),
                pl.BlockSpec((TAIL, TILE), lane),
                pl.BlockSpec((4, TILE), lane),
                pl.BlockSpec((1, TILE), lane),
                pl.BlockSpec(wabs.shape, still),
                pl.BlockSpec((1, spread.shape[1], TILE), lambda j, core: (group_of(turn, core), 0, half * tiles + j)),
                pl.BlockSpec(tot.shape, still),
                *ends,
            ],
            out_specs=[pl.BlockSpec((rows, STATE), still)] * fresh
            + [pl.BlockSpec((rows, TILE), out), pl.BlockSpec((STATE + EXTRA, TILE), out)],
            scratch_shapes=[
                pltpu.VMEM((rows + 8, 128), F32),
                pltpu.VMEM((rows, TILE), BF16),
                pltpu.VMEM((STATE, rows), BF16),
            ],
        ),
        out_shape=[jax.ShapeDtypeStruct((rows, STATE), BF16)] * fresh
        + [
            jax.ShapeDtypeStruct((rows, width), BF16),
            jax.ShapeDtypeStruct((STATE + EXTRA, width), BF16),
        ],
        compiler_params=params("arbitrary"),
        cost_estimate=pl.CostEstimate(
            flops=2 * rows * STATE * width, bytes_accessed=4 * rows * width, transcendentals=rows * width
        ),
    )(core, x, tails, wx, ox, wabs, spread, tot, *last)


def values_kernel(
    core_ref, x_ref, b_ref, c_ref, run_ref, row_ref, ehl_ref, whl_ref, spread_ref, sent_ref, out_ref, done_ref, near, inside, across
):
    done_ref[0] = 0
    rows = x_ref.shape[0]
    blocks = rows // BLOCK
    part = lambda n: slice(n * CHUNK, (n + 1) * CHUNK)
    whole = lambda n: slice(n * BLOCK, (n + 1) * BLOCK)
    pairs = [(late, early) for late in range(blocks) for early in range(late)]

    @pl.when(pl.program_id(0) == 0)
    def _():
        t = lax.broadcasted_iota(jnp.int32, (CHUNK, CHUNK), 0)
        s = lax.broadcasted_iota(jnp.int32, (CHUNK, CHUNK), 1)
        for n in range(2 * blocks):
            near[n] = jnp.where(t >= s, dot(c_ref[part(n), :], b_ref[part(n), :], 1, 1), 0.0)
        for n in range(blocks):
            inside[n] = dot(c_ref[part(2 * n + 1), :], b_ref[part(2 * n), :], 1, 1).astype(BF16)
        for n, (late, early) in enumerate(pairs):
            across[n] = dot(c_ref[whole(late), :], b_ref[whole(early), :], 1, 1).astype(BF16)

    left = lax.broadcasted_iota(jnp.int32, (CHUNK, 128), 1) < HEAD_DIM
    turned = [run_ref[:, part(n)].T for n in range(2 * blocks)]
    for lane in range(0, VTILE, 256):
        cut = slice(lane, lane + 256)
        spread = spread_ref[0, :, cut]
        sent, faded = [], []
        for n in range(blocks):
            grown = dot(ehl_ref[whole(n), :], spread)
            weight = dot(whl_ref[whole(n), :], spread)
            x = x_ref[whole(n), cut].astype(F32)
            early_fade = grown[CHUNK - 1 : CHUNK, :]
            late_fade = grown[BLOCK - 1 : BLOCK, :]
            scaled = weight * x
            ended = jnp.concatenate([scaled[:CHUNK] * late_fade, scaled[CHUNK:]], axis=0).astype(BF16)
            sent.append(ended)
            faded.append(early_fade * late_fade)
            carried = None
            for early in range(n):
                came = dot(across[pairs.index((n, early))], sent[early])
                carried = came if carried is None else carried * faded[early] + came
            second = dot(inside[n], scaled[:CHUNK].astype(BF16))
            if carried is not None:
                second = second + carried[CHUNK:] * early_fade
            from_before = (None if carried is None else carried[:CHUNK], second)
            for side in range(2):
                m = 2 * n + side
                base = near[m]
                for pair in range(2):
                    first = lane // HEAD_DIM + 2 * pair
                    low = lane + 128 * pair
                    mixes = []
                    for h in (first, first + 1):
                        along = turned[m][:, h : h + 1] - row_ref[h : h + 1, part(m)]
                        mixes.append((base * jnp.exp2(jnp.minimum(along, 64.0))).astype(BF16))
                    xs = x_ref[part(m), low : low + 128]
                    none = jnp.zeros_like(xs)
                    sides = jnp.concatenate([jnp.where(left, xs, none), jnp.where(left, none, xs)], axis=0)
                    total = dot(jnp.concatenate(mixes, axis=1), sides)
                    if from_before[side] is not None:
                        own = slice(128 * pair, 128 * pair + 128)
                        total = total + grown[side * CHUNK : (side + 1) * CHUNK, own] * from_before[side][:, own]
                    out_ref[part(m), low : low + 128] = total.astype(out_ref.dtype)


def local_values(turn, half, core, x, b, c, run, row, ehl, whl, spread, sent):
    rows, width = x.shape
    blocks = rows // BLOCK
    tiles = width // VTILE
    heads = VTILE // HEAD_DIM
    head = lambda j, core: ((group_of(turn, core) * HALVES + half) * tiles + j, 0)
    still = lambda j, core: (0, 0)
    lane = lambda j, core: (0, j)
    return pl.pallas_call(
        values_kernel,
        grid_spec=pltpu.PrefetchScalarGridSpec(
            num_scalar_prefetch=1,
            grid=(tiles,),
            in_specs=[
                pl.BlockSpec((rows, VTILE), lane),
                pl.BlockSpec((rows, STATE), still),
                pl.BlockSpec((rows, STATE), still),
                pl.BlockSpec((heads, rows), head),
                pl.BlockSpec((heads, rows), head),
                pl.BlockSpec(ehl.shape, still),
                pl.BlockSpec(whl.shape, still),
                pl.BlockSpec((1, spread.shape[1], VTILE), lambda j, core: (group_of(turn, core), 0, half * tiles + j)),
                pl.BlockSpec(memory_space=pl.ANY),
            ],
            out_specs=[pl.BlockSpec((rows, VTILE), lane), pl.BlockSpec(memory_space=pltpu.SMEM)],
            scratch_shapes=[
                pltpu.VMEM((2 * blocks, CHUNK, CHUNK), F32),
                pltpu.VMEM((blocks, CHUNK, CHUNK), BF16),
                pltpu.VMEM((blocks * (blocks - 1) // 2, BLOCK, BLOCK), BF16),
            ],
        ),
        out_shape=[jax.ShapeDtypeStruct((rows, width), BF16), jax.ShapeDtypeStruct((1,), jnp.int32)],
        compiler_params=params("arbitrary"),
        cost_estimate=pl.CostEstimate(
            flops=8 * rows * STATE * width, bytes_accessed=8 * rows * width, transcendentals=rows * CHUNK * width // HEAD_DIM
        ),
    )(core, x, b, c, run, row, ehl, whl, spread, sent)


def norm_kernel(core_ref, c_ref, eabs_ref, spread_ref, z_ref, gain_ref, reward_ref, *rest):
    values, states = rest[:HALVES], rest[HALVES : 2 * HALVES]
    out_ref, term_ref, gated = rest[-3:]
    rows = c_ref.shape[0]
    c = c_ref[...]
    decay = eabs_ref[...]
    squares = jnp.zeros((rows, 128), F32)
    for lane in range(0, LANES, 256):
        cut = slice(lane, lane + 256)
        half, low = divmod(lane, LANES // HALVES)
        own = slice(low, low + 256)
        v = values[half][:, own].astype(F32) + dot(decay, spread_ref[0, :, cut]) * dot(c, states[half][:, own])
        v = v * silu(z_ref[:, cut].astype(F32))
        gated[:, cut] = v
        squares = squares + v[:, :128] * v[:, :128] + v[:, 128:] * v[:, 128:]
    scale = lax.rsqrt(jnp.sum(squares, axis=1, keepdims=True) * (1.0 / LANES) + 1e-05)
    terms = jnp.zeros((rows, 128), F32)
    for lane in range(0, LANES, 128):
        cut = slice(lane, lane + 128)
        v = (gated[:, cut] * scale * gain_ref[:, cut]).astype(BF16)
        out_ref[:, cut] = v
        terms = terms + v.astype(F32) * reward_ref[:, cut]
    term_ref[...] = terms


def gated_norm(turn, core, values, c, states, eabs, spread, z, gain, reward, target):
    rows = c.shape[0]
    width = LANES // HALVES
    own = lambda i, core: (i, group_of(turn, core))
    side = lambda i, core: (0, group_of(turn, core))
    down = lambda i, core: (i, 0)
    still = lambda i, core: (0, 0)
    return pl.pallas_call(
        norm_kernel,
        grid_spec=pltpu.PrefetchScalarGridSpec(
            num_scalar_prefetch=1,
            grid=(rows // ROWS,),
            in_specs=[
                pl.BlockSpec((ROWS, STATE), down),
                pl.BlockSpec((ROWS, eabs.shape[1]), down),
                pl.BlockSpec((1, spread.shape[1], LANES), lambda i, core: (group_of(turn, core), 0, 0)),
                pl.BlockSpec((ROWS, LANES), own),
                pl.BlockSpec((1, LANES), side),
                pl.BlockSpec((1, LANES), side),
            ]
            + [pl.BlockSpec((ROWS, width), down)] * HALVES
            + [pl.BlockSpec((STATE, width), still)] * HALVES
            + ([] if target is None else [pl.BlockSpec(memory_space=pl.ANY)]),
            out_specs=[pl.BlockSpec((ROWS, LANES), own), pl.BlockSpec((ROWS, 128), down)],
            scratch_shapes=[pltpu.VMEM((ROWS, LANES), F32)],
        ),
        out_shape=[jax.ShapeDtypeStruct(z.shape, BF16), jax.ShapeDtypeStruct((rows, 128), F32)],
        input_output_aliases={} if target is None else {7 + 2 * HALVES: 0},
        compiler_params=params("arbitrary"),
        cost_estimate=pl.CostEstimate(
            flops=2 * rows * STATE * LANES, bytes_accessed=8 * rows * LANES, transcendentals=rows * LANES
        ),
    )(core, c, eabs, spread, z, gain, reward, *values, *states, *(() if target is None else (target,)))


def total_of(payload):
    extra = payload[STATE : STATE + 3].astype(F32)
    return extra[0:1] + extra[1:2] + extra[2:3]


def with_total(state, total):
    rows = jnp.concatenate(split3(total), axis=0)
    rows = jnp.pad(rows, ((0, EXTRA - 3), (0, 0)))
    return jnp.concatenate([state.astype(BF16), rows], axis=0)


def advance(state, payload):
    return jnp.exp2(total_of(payload)) * state + payload[:STATE].astype(F32)


def over(value, move):
    count = lax.axis_size("seq")
    return lax.ppermute(value, "seq", [(i, move(i)) for i in range(count) if move(i) is not None])


def along_y(k):
    return lambda i: i // 8 * 8 + (i // 2 + k) % 4 * 2 + i % 2


def entering_state(away, mine):
    place = lax.axis_index("seq")
    core = place % 2
    y = place // 2 % 4
    other = over(away, lambda i: i ^ 1)
    first = jnp.where(core == 0, mine, other)
    second = jnp.where(core == 0, other, mine)
    chip = with_total(
        advance(first[:STATE].astype(F32), second), total_of(first) + total_of(second)
    )
    quarter = chip.shape[1] // 4
    piece = lambda n: lax.dynamic_slice_in_dim(chip, n * quarter, quarter, 1)
    going = [piece((y + k) % 4) for k in range(4)]
    came = jnp.stack([going[0]] + [over(going[k], along_y(k)) for k in (1, 2, 3)])
    y = y + (yield going[3])
    parts = [lax.dynamic_index_in_dim(came, (y - n) % 4, 0, False) for n in range(4)]
    state, total = parts[0][:STATE].astype(F32), total_of(parts[0])
    for n in range(1, 4):
        state, total = advance(state, parts[n]), total + total_of(parts[n])
    row = with_total(state, total)
    near, mid, far = (
        over(row, lambda i, k=k: i + 8 * k if i + 8 * k < 32 else None) for k in (1, 2, 3)
    )
    state = advance(advance(far[:STATE].astype(F32), mid), near)
    entering = []
    for n in range(4):
        entering.append(state.astype(BF16))
        state = advance(state, parts[n])
    entering = jnp.stack(entering)
    going = [lax.dynamic_index_in_dim(entering, (y + k) % 4, 0, False) for k in range(4)]
    back = jnp.stack([going[0]] + [over(going[k], along_y(k)) for k in (1, 2, 3)])
    y = y + (yield going[3])
    chip_in = jnp.concatenate(
        [lax.dynamic_index_in_dim(back, (y - n) % 4, 0, False) for n in range(4)], axis=1
    )
    later = advance(chip_in.astype(F32), first).astype(BF16)
    got = over(jnp.where(core == 0, later, chip_in), lambda i: i ^ 1)
    yield got, jnp.where(core == 0, chip_in, later)


def per_device(
    x_in, z_in, bc_in, dt_in, conv_x_weight, conv_x_bias, conv_bc_weight, conv_bc_bias,
    dt_bias, a_log, norm_gain, reward_w, step_ends,
):
    rows = x_in.shape[0]
    place = lax.axis_index("seq")
    core = (place % 2).reshape(1)
    bc = bc_in.reshape(rows, -1)
    tails = jnp.concatenate([x_in[rows - TAIL :], bc_in[rows - TAIL :].reshape(TAIL, -1)], axis=1)
    tails = over(tails, lambda i: i + 1 if i + 1 < 32 else None)
    run, row, ehl, whl, eabs, wabs, tot = decays(dt_in.T, dt_bias[None], a_log[None])
    heads = dt_in.shape[1]
    groups = heads // PER_GROUP
    head = np.arange(heads * HEAD_DIM).reshape(groups, 1, LANES) // HEAD_DIM
    spread = jnp.asarray(np.arange(2 * heads)[:, None] % heads == head, BF16)
    wx, ox = conv_x_weight, conv_x_bias[None]
    made = [[], []]
    for half in range(HALVES):
        for turn in range(2):
            made[turn].append(
                local_states(
                    turn, half, core, x_in, tails, wx, ox, wabs, spread, tot, bc, conv_bc_weight, conv_bc_bias,
                    made[turn][0][0] if half else None,
                )
            )
    values = [[], []]

    def inner(turn, sent):
        m = made[turn]
        done = None
        for half in range(HALVES):
            v, done = local_values(
                turn, half, core, m[half][-2], m[0][0], m[0][1], run, row, ehl, whl, spread, sent
            )
            values[turn].append(v)
        return done[0]

    steps = entering_state(made[0][0][-1], made[1][0][-1])
    sent = next(steps)
    sent = steps.send(inner(1, sent))
    entered = [steps.send(inner(0, sent))]
    normed, sums = None, []
    for turn in (1, 0):
        normed, part = gated_norm(
            turn, core, values[turn], made[turn][0][1], [e[turn] for e in entered], eabs, spread, z_in,
            norm_gain[None], reward_w[None], normed,
        )
        sums.append(part)
    local_pos = step_ends - place * rows
    inside = (local_pos >= 0) & (local_pos < rows)
    at = jnp.clip(local_pos, 0, rows - 1)
    terms = jnp.sum(jnp.take(sums[0], at, axis=0) + jnp.take(sums[1], at, axis=0), axis=1)
    terms = jnp.where(inside, terms, 0.0)
    devices = lax.axis_size("seq") * lax.axis_size("head")
    terms = lax.all_to_all(jnp.broadcast_to(terms, (devices, terms.shape[0])), ("seq", "head"), 0, 0)
    return normed, jnp.sum(terms, axis=0)


def solution(mesh):
    return jax.shard_map(
        per_device,
        mesh=mesh,
        in_specs=(
            P("seq", "head"),
            P("seq", "head"),
            P("seq", None, "head"),
            P("seq", "head"),
            P(None, "head"),
            P("head"),
            P(None, None, "head"),
            P(None, "head"),
            P("head"),
            P("head"),
            P("head"),
            P("head"),
            P(),
        ),
        out_specs=(P("seq", "head"), P()),
        check_vma=False,
    )
```

```python
import functools

import jax
import jax.numpy as jnp
import numpy as np
from jax import lax
from jax.experimental import pallas as pl
from jax.experimental.pallas import tpu as pltpu
from jax.sharding import PartitionSpec as P

HEAD_DIM = 64
STATE = 256
PER_GROUP = 32
LANES = PER_GROUP * HEAD_DIM
CHUNK = 128
TAIL = 16
EXTRA = 16
TILE = 512
ROWS = 256
BLOCK = 2 * CHUNK
VTILE = 512
HALVES = 1
LOG2E = 1.4426950408889634
F32 = jnp.float32
BF16 = jnp.bfloat16
VMEM_LIMIT = 56 * 1024 * 1024


def params(*semantics):
    return pltpu.CompilerParams(
        dimension_semantics=semantics or None, vmem_limit_bytes=VMEM_LIMIT
    )


def dot(a, b, ca=1, cb=0):
    return lax.dot_general(a, b, (((ca,), (cb,)), ((), ())), preferred_element_type=F32)


def split2(v):
    high = v.astype(BF16)
    return high, (v - high.astype(F32)).astype(BF16)


def split3(v):
    high = v.astype(BF16)
    rest = v - high.astype(F32)
    mid = rest.astype(BF16)
    return high, mid, (rest - mid.astype(F32)).astype(BF16)


def silu_of_twice(half):
    return half + half * jnp.tanh(half)


def silu(v):
    return silu_of_twice(0.5 * v)


def decay_kernel(
    dtin_ref, bias_ref, alog_ref, run_ref, row_ref, ehl_ref, whl_ref, eabs_ref, wabs_ref, tot_ref
):
    heads, rows = dtin_ref.shape
    count = rows // CHUNK
    h0 = lax.broadcasted_iota(jnp.int32, (heads, heads), 0)
    h1 = lax.broadcasted_iota(jnp.int32, (heads, heads), 1)
    upright = lambda v: jnp.sum(jnp.where(h0 == h1, v, 0.0), axis=1, keepdims=True)
    bias = upright(bias_ref[...])
    rate = upright(-LOG2E * jnp.exp(alog_ref[...]))
    u = lax.broadcasted_iota(jnp.int32, (CHUNK, CHUNK), 0)
    t = lax.broadcasted_iota(jnp.int32, (CHUNK, CHUNK), 1)
    upto = (u <= t).astype(BF16)
    after = (u > t).astype(BF16)
    steps, running, suffix, kept = [], [], [], []
    for c in range(count):
        v = dtin_ref[:, c * CHUNK : (c + 1) * CHUNK] + bias
        dt = jnp.maximum(v, 0.0) + jnp.log1p(jnp.exp(-jnp.abs(v)))
        terms = jnp.concatenate(split3(dt * rate), axis=0)
        r = dot(terms, upto)
        s = dot(terms, after)
        r = r[:heads] + r[heads : 2 * heads] + r[2 * heads :]
        s = s[:heads] + s[heads : 2 * heads] + s[2 * heads :]
        steps.append(dt)
        running.append(r)
        suffix.append(s)
    def put(ref, v, c):
        where = slice(c * CHUNK, (c + 1) * CHUNK)
        ref[where, 0:heads], ref[where, heads : 2 * heads] = split2(v)

    whole = jnp.zeros((1, heads), F32)
    for c in range(count):
        where = slice(c * CHUNK, (c + 1) * CHUNK)
        run_ref[:, where] = running[c]
        row_ref[:, where] = running[c] - jnp.log2(steps[c])
        run, rest, dt = running[c].T, suffix[c].T, steps[c].T
        grown, weight = jnp.exp2(run), jnp.exp2(rest) * dt
        put(ehl_ref, grown, c)
        put(whl_ref, weight, c)
        put(eabs_ref, grown * jnp.exp2(whole), c)
        whole = whole + run[CHUNK - 1 :, :]
        kept.append((weight, run[CHUNK - 1 :, :]))
    later = jnp.zeros((1, heads), F32)
    for c in range(count - 1, -1, -1):
        put(wabs_ref, kept[c][0] * jnp.exp2(later), c)
        later = later + kept[c][1]
    high, mid, low = split3(whole)
    place = lax.broadcasted_iota(jnp.int32, (EXTRA, heads), 0)
    terms = jnp.where(
        place == 0,
        high.astype(F32),
        jnp.where(place == 1, mid.astype(F32), jnp.where(place == 2, low.astype(F32), 0.0)),
    ).astype(BF16)
    tot_ref[:, 0:heads] = terms
    tot_ref[:, heads : 2 * heads] = jnp.zeros_like(terms)


def decays(dt_in, bias, a_log):
    heads, rows = dt_in.shape
    pair = jax.ShapeDtypeStruct((rows, 2 * heads), BF16)
    return pl.pallas_call(
        decay_kernel,
        out_shape=[
            jax.ShapeDtypeStruct((heads, rows), F32),
            jax.ShapeDtypeStruct((heads, rows), F32),
            pair,
            pair,
            pair,
            pair,
            jax.ShapeDtypeStruct((EXTRA, 2 * heads), BF16),
        ],
        compiler_params=params(),
        cost_estimate=pl.CostEstimate(flops=10**8, bytes_accessed=2 * 10**6, transcendentals=heads * rows * 5),
    )(dt_in, bias, a_log)


def load_column(pad, series, tail):
    pad[0:8, :] = tail[...].astype(F32)[TAIL - 8 :]
    pad[8 : 8 + series.shape[0], :] = series[...].astype(F32)


def conv_rows(pad, start, taps, offset):
    total = offset + taps[3] * pad[8 + start : 8 + start + CHUNK, :]
    for k in range(3):
        total = total + taps[k] * pad[5 + k + start : 5 + k + start + CHUNK, :]
    return silu_of_twice(total).astype(BF16)


def state_kernel(core_ref, x_ref, xt_ref, wx_ref, ox_ref, wabs_ref, spread_ref, tot_ref, *rest):
    rows = x_ref.shape[0]
    cx_ref, state_ref, pad, scaled, bturn = rest[-5:]
    if len(rest) == 6:
        made_ref = rest[0]

        @pl.when(pl.program_id(0) == 0)
        def _():
            bturn[...] = made_ref[...].T

    else:
        b_ref, bt_ref, c_ref, ct_ref, wb_ref, ob_ref, cb_ref, cc_ref = rest[:8]

        @pl.when(pl.program_id(0) == 0)
        def _():
            for n, (src, tail, dst) in enumerate(((b_ref, bt_ref, cb_ref), (c_ref, ct_ref, cc_ref))):
                for lane in range(0, STATE, 128):
                    own = slice(lane, lane + 128)
                    load_column(pad.at[0], src.at[:, own], tail.at[:, own])
                    taps = [0.5 * wb_ref[k, n : n + 1, own] for k in range(4)]
                    offset = 0.5 * ob_ref[n : n + 1, own]
                    for start in range(0, rows, CHUNK):
                        dst[start : start + CHUNK, own] = conv_rows(pad.at[0], start, taps, offset)
            bturn[...] = cb_ref[...].T

    for lane in range(0, TILE, 256):
        sides = [slice(lane + 128 * n, lane + 128 * n + 128) for n in range(2)]
        for n, own in enumerate(sides):
            load_column(pad.at[n], x_ref.at[:, own], xt_ref.at[:, own])
        taps = [[0.5 * wx_ref[k : k + 1, own] for k in range(4)] for own in sides]
        offsets = [0.5 * ox_ref[:, own] for own in sides]
        for start in range(0, rows, CHUNK):
            here = slice(start, start + CHUNK)
            w = dot(wabs_ref[here, :], spread_ref[0, :, lane : lane + 256])
            for n, own in enumerate(sides):
                v = conv_rows(pad.at[n], start, taps[n], offsets[n])
                cx_ref[here, own] = v
                scaled[here, own] = (w[:, 128 * n : 128 * n + 128] * v.astype(F32)).astype(BF16)
    state_ref[0:STATE, :] = dot(bturn[...], scaled[...]).astype(BF16)
    state_ref[STATE:, :] = dot(tot_ref[...], spread_ref[0]).astype(BF16)


def group_of(turn, core):
    own = lax.rem(core[0], 2)
    return own if turn else 1 - own


def local_states(turn, half, core, x, tails, wx, ox, wabs, spread, tot, bc, wbc, obc, made=None):
    rows, channels = x.shape
    groups = channels // LANES
    width = LANES // HALVES
    tiles = width // TILE
    first = channels // STATE
    lane = lambda j, core: (0, (group_of(turn, core) * HALVES + half) * tiles + j)
    own = lambda shift: lambda j, core: (0, shift + group_of(turn, core))
    still = lambda j, core: (0, 0)
    out = lambda j, core: (0, j)
    if made is None:
        ends = [
            pl.BlockSpec((rows, STATE), own(0)),
            pl.BlockSpec((TAIL, STATE), own(first)),
            pl.BlockSpec((rows, STATE), own(groups)),
            pl.BlockSpec((TAIL, STATE), own(first + groups)),
            pl.BlockSpec((4, 2, STATE), lambda j, core: (0, 0, group_of(turn, core))),
            pl.BlockSpec((2, STATE), own(0)),
        ]
        last = (bc, tails, bc, tails, wbc, obc)
    else:
        ends = [pl.BlockSpec((rows, STATE), still)]
        last = (made,)
    fresh = 2 if made is None else 0
    return pl.pallas_call(
        state_kernel,
        grid_spec=pltpu.PrefetchScalarGridSpec(
            num_scalar_prefetch=1,
            grid=(tiles,),
            in_specs=[
                pl.BlockSpec((rows, TILE), lane),
                pl.BlockSpec((TAIL, TILE), lane),
                pl.BlockSpec((4, TILE), lane),
                pl.BlockSpec((1, TILE), lane),
                pl.BlockSpec(wabs.shape, still),
                pl.BlockSpec((1, spread.shape[1], TILE), lambda j, core: (group_of(turn, core), 0, half * tiles + j)),
                pl.BlockSpec(tot.shape, still),
                *ends,
            ],
            out_specs=[pl.BlockSpec((rows, STATE), still)] * fresh
            + [pl.BlockSpec((rows, TILE), out), pl.BlockSpec((STATE + EXTRA, TILE), out)],
            scratch_shapes=[
                pltpu.VMEM((2, rows + 8, 128), F32),
                pltpu.VMEM((rows, TILE), BF16),
                pltpu.VMEM((STATE, rows), BF16),
            ],
        ),
        out_shape=[jax.ShapeDtypeStruct((rows, STATE), BF16)] * fresh
        + [
            jax.ShapeDtypeStruct((rows, width), BF16),
            jax.ShapeDtypeStruct((STATE + EXTRA, width), BF16),
        ],
        compiler_params=params("arbitrary"),
        cost_estimate=pl.CostEstimate(
            flops=2 * rows * STATE * width, bytes_accessed=4 * rows * width, transcendentals=rows * width
        ),
    )(core, x, tails, wx, ox, wabs, spread, tot, *last)


def values_kernel(
    core_ref, x_ref, b_ref, c_ref, run_ref, row_ref, ehl_ref, whl_ref, spread_ref, sent_ref, out_ref, done_ref, near, inside, across
):
    done_ref[0] = 0
    rows = x_ref.shape[0]
    blocks = rows // BLOCK
    part = lambda n: slice(n * CHUNK, (n + 1) * CHUNK)
    whole = lambda n: slice(n * BLOCK, (n + 1) * BLOCK)
    pairs = [(late, early) for late in range(blocks) for early in range(late)]

    @pl.when(pl.program_id(0) == 0)
    def _():
        t = lax.broadcasted_iota(jnp.int32, (CHUNK, CHUNK), 0)
        s = lax.broadcasted_iota(jnp.int32, (CHUNK, CHUNK), 1)
        for n in range(2 * blocks):
            near[n] = jnp.where(t >= s, dot(c_ref[part(n), :], b_ref[part(n), :], 1, 1), 0.0)
        for n in range(blocks):
            inside[n] = dot(c_ref[part(2 * n + 1), :], b_ref[part(2 * n), :], 1, 1).astype(BF16)
        for n, (late, early) in enumerate(pairs):
            across[n] = dot(c_ref[whole(late), :], b_ref[whole(early), :], 1, 1).astype(BF16)

    left = lax.broadcasted_iota(jnp.int32, (CHUNK, 128), 1) < HEAD_DIM
    turned = [run_ref[:, part(n)].T for n in range(2 * blocks)]
    for lane in range(0, VTILE, 256):
        cut = slice(lane, lane + 256)
        spread = spread_ref[0, :, cut]
        sent, faded = [], []
        for n in range(blocks):
            grown = dot(ehl_ref[whole(n), :], spread)
            weight = dot(whl_ref[whole(n), :], spread)
            x = x_ref[whole(n), cut].astype(F32)
            early_fade = grown[CHUNK - 1 : CHUNK, :]
            late_fade = grown[BLOCK - 1 : BLOCK, :]
            scaled = weight * x
            ended = jnp.concatenate([scaled[:CHUNK] * late_fade, scaled[CHUNK:]], axis=0).astype(BF16)
            sent.append(ended)
            faded.append(early_fade * late_fade)
            carried = None
            for early in range(n):
                came = dot(across[pairs.index((n, early))], sent[early])
                carried = came if carried is None else carried * faded[early] + came
            second = dot(inside[n], scaled[:CHUNK].astype(BF16))
            if carried is not None:
                second = second + carried[CHUNK:] * early_fade
            from_before = (None if carried is None else carried[:CHUNK], second)
            for side in range(2):
                m = 2 * n + side
                base = near[m]
                for pair in range(2):
                    first = lane // HEAD_DIM + 2 * pair
                    low = lane + 128 * pair
                    mixes = []
                    for h in (first, first + 1):
                        along = turned[m][:, h : h + 1] - row_ref[h : h + 1, part(m)]
                        mixes.append((base * jnp.exp2(jnp.minimum(along, 64.0))).astype(BF16))
                    xs = x_ref[part(m), low : low + 128]
                    none = jnp.zeros_like(xs)
                    sides = jnp.concatenate([jnp.where(left, xs, none), jnp.where(left, none, xs)], axis=0)
                    total = dot(jnp.concatenate(mixes, axis=1), sides)
                    if from_before[side] is not None:
                        own = slice(128 * pair, 128 * pair + 128)
                        total = total + grown[side * CHUNK : (side + 1) * CHUNK, own] * from_before[side][:, own]
                    out_ref[part(m), low : low + 128] = total.astype(out_ref.dtype)


def local_values(turn, half, core, x, b, c, run, row, ehl, whl, spread, sent):
    rows, width = x.shape
    blocks = rows // BLOCK
    tiles = width // VTILE
    heads = VTILE // HEAD_DIM
    head = lambda j, core: ((group_of(turn, core) * HALVES + half) * tiles + j, 0)
    still = lambda j, core: (0, 0)
    lane = lambda j, core: (0, j)
    return pl.pallas_call(
        values_kernel,
        grid_spec=pltpu.PrefetchScalarGridSpec(
            num_scalar_prefetch=1,
            grid=(tiles,),
            in_specs=[
                pl.BlockSpec((rows, VTILE), lane),
                pl.BlockSpec((rows, STATE), still),
                pl.BlockSpec((rows, STATE), still),
                pl.BlockSpec((heads, rows), head),
                pl.BlockSpec((heads, rows), head),
                pl.BlockSpec(ehl.shape, still),
                pl.BlockSpec(whl.shape, still),
                pl.BlockSpec((1, spread.shape[1], VTILE), lambda j, core: (group_of(turn, core), 0, half * tiles + j)),
                pl.BlockSpec(memory_space=pl.ANY),
            ],
            out_specs=[pl.BlockSpec((rows, VTILE), lane), pl.BlockSpec(memory_space=pltpu.SMEM)],
            scratch_shapes=[
                pltpu.VMEM((2 * blocks, CHUNK, CHUNK), F32),
                pltpu.VMEM((blocks, CHUNK, CHUNK), BF16),
                pltpu.VMEM((blocks * (blocks - 1) // 2, BLOCK, BLOCK), BF16),
            ],
        ),
        out_shape=[jax.ShapeDtypeStruct((rows, width), BF16), jax.ShapeDtypeStruct((1,), jnp.int32)],
        compiler_params=params("arbitrary"),
        cost_estimate=pl.CostEstimate(
            flops=8 * rows * STATE * width, bytes_accessed=8 * rows * width, transcendentals=rows * CHUNK * width // HEAD_DIM
        ),
    )(core, x, b, c, run, row, ehl, whl, spread, sent)


def norm_kernel(
    devices, place_ref, c_ref, state_ref, values_ref, z_ref, eabs_ref, spread_ref, gain_ref, reward_ref, ends_ref, *rest
):
    earlier = rest[0] if devices else None
    out_ref, term_ref, gated, sums = rest[-4:]
    rows = c_ref.shape[0]
    step = pl.program_id(0)
    c = c_ref[...]
    decay = eabs_ref[...]
    squares = jnp.zeros((rows, 128), F32)
    for lane in range(0, LANES, 256):
        cut = slice(lane, lane + 256)
        v = values_ref[:, cut].astype(F32) + dot(decay, spread_ref[0, :, cut]) * dot(c, state_ref[:, cut])
        v = v * silu(z_ref[:, cut].astype(F32))
        gated[:, cut] = v
        squares = squares + v[:, :128] * v[:, :128] + v[:, 128:] * v[:, 128:]
    scale = lax.rsqrt(jnp.sum(squares, axis=1, keepdims=True) * (1.0 / LANES) + 1e-05)
    terms = jnp.zeros((rows, 128), F32)
    for lane in range(0, LANES, 128):
        cut = slice(lane, lane + 128)
        v = (gated[:, cut] * scale * gain_ref[:, cut]).astype(BF16)
        out_ref[:, cut] = v
        terms = terms + v.astype(F32) * reward_ref[:, cut]
    if devices:
        first = (place_ref[0] * pl.num_programs(0) + step) * rows
        row = lax.broadcasted_iota(jnp.int32, (rows, ends_ref.shape[1]), 0)
        term = jnp.sum(terms + earlier[...], axis=1, keepdims=True)
        found = jnp.where(row == ends_ref[...] - first, term, 0.0)
        found = jnp.sum(found, axis=0, keepdims=True)

        @pl.when(step == 0)
        def _():
            sums[...] = jnp.zeros_like(sums)

        sums[0:1, :] = sums[0:1, :] + found

        @pl.when(step == pl.num_programs(0) - 1)
        def _():
            term_ref[...] = jnp.broadcast_to(sums[0:1, :], term_ref.shape)

    else:
        term_ref[...] = terms


def gated_norm(turn, core, values, c, state, eabs, spread, z, gain, reward, ends, earlier=None, devices=0):
    rows = c.shape[0]
    count = ends.shape[1]
    own = lambda i, core: (i, group_of(turn, core))
    side = lambda i, core: (0, group_of(turn, core))
    down = lambda i, core: (i, 0)
    still = lambda i, core: (0, 0)
    more = [pl.BlockSpec((ROWS, 128), down), pl.BlockSpec(memory_space=pl.ANY)] if devices else []
    terms = (devices, count) if devices else (rows, 128)
    return pl.pallas_call(
        functools.partial(norm_kernel, devices),
        grid_spec=pltpu.PrefetchScalarGridSpec(
            num_scalar_prefetch=1,
            grid=(rows // ROWS,),
            in_specs=[
                pl.BlockSpec((ROWS, STATE), down),
                pl.BlockSpec((STATE, LANES), still),
                pl.BlockSpec((ROWS, LANES), down),
                pl.BlockSpec((ROWS, LANES), own),
                pl.BlockSpec((ROWS, eabs.shape[1]), down),
                pl.BlockSpec((1, spread.shape[1], LANES), lambda i, core: (group_of(turn, core), 0, 0)),
                pl.BlockSpec((1, LANES), side),
                pl.BlockSpec((1, LANES), side),
                pl.BlockSpec((1, count), still),
            ]
            + more,
            out_specs=[
                pl.BlockSpec((ROWS, LANES), own),
                pl.BlockSpec(terms, still) if devices else pl.BlockSpec((ROWS, 128), down),
            ],
            scratch_shapes=[pltpu.VMEM((ROWS, LANES), F32), pltpu.VMEM((8, count), F32)],
        ),
        out_shape=[jax.ShapeDtypeStruct(z.shape, BF16), jax.ShapeDtypeStruct(terms, F32)],
        input_output_aliases={11: 0} if devices else {},
        compiler_params=params("arbitrary"),
        cost_estimate=pl.CostEstimate(
            flops=2 * rows * STATE * LANES, bytes_accessed=6 * rows * LANES, transcendentals=rows * LANES
        ),
    )(core, c, state, values, z, eabs, spread, gain, reward, ends, *(earlier or ()))


def total_of(payload):
    extra = payload[STATE : STATE + 3].astype(F32)
    return extra[0:1] + extra[1:2] + extra[2:3]


def with_total(state, total):
    rows = jnp.concatenate(split3(total), axis=0)
    rows = jnp.pad(rows, ((0, EXTRA - 3), (0, 0)))
    return jnp.concatenate([state.astype(BF16), rows], axis=0)


def advance(state, payload):
    return jnp.exp2(total_of(payload)) * state + payload[:STATE].astype(F32)


def over(value, move):
    count = lax.axis_size("seq")
    return lax.ppermute(value, "seq", [(i, move(i)) for i in range(count) if move(i) is not None])


def along_y(k):
    return lambda i: i // 8 * 8 + (i // 2 + k) % 4 * 2 + i % 2


def entering_state(away, mine):
    place = lax.axis_index("seq")
    core = place % 2
    y = place // 2 % 4
    other = over(away, lambda i: i ^ 1)
    first = jnp.where(core == 0, mine, other)
    second = jnp.where(core == 0, other, mine)
    chip = with_total(
        advance(first[:STATE].astype(F32), second), total_of(first) + total_of(second)
    )
    quarter = chip.shape[1] // 4
    piece = lambda n: lax.dynamic_slice_in_dim(chip, n * quarter, quarter, 1)
    going = [piece((y + k) % 4) for k in range(4)]
    came = jnp.stack([going[0]] + [over(going[k], along_y(k)) for k in (1, 2, 3)])
    y = y + (yield going[3])
    parts = [lax.dynamic_index_in_dim(came, (y - n) % 4, 0, False) for n in range(4)]
    state, total = parts[0][:STATE].astype(F32), total_of(parts[0])
    for n in range(1, 4):
        state, total = advance(state, parts[n]), total + total_of(parts[n])
    row = with_total(state, total)
    near, mid, far = (
        over(row, lambda i, k=k: i + 8 * k if i + 8 * k < 32 else None) for k in (1, 2, 3)
    )
    state = advance(advance(far[:STATE].astype(F32), mid), near)
    entering = []
    for n in range(4):
        entering.append(state.astype(BF16))
        state = advance(state, parts[n])
    entering = jnp.stack(entering)
    going = [lax.dynamic_index_in_dim(entering, (y + k) % 4, 0, False) for k in range(4)]
    back = jnp.stack([going[0]] + [over(going[k], along_y(k)) for k in (1, 2, 3)])
    y = y + (yield going[3])
    chip_in = jnp.concatenate(
        [lax.dynamic_index_in_dim(back, (y - n) % 4, 0, False) for n in range(4)], axis=1
    )
    later = advance(chip_in.astype(F32), first).astype(BF16)
    got = over(jnp.where(core == 0, later, chip_in), lambda i: i ^ 1)
    yield got, jnp.where(core == 0, chip_in, later)


def per_device(
    x_in, z_in, bc_in, dt_in, conv_x_weight, conv_x_bias, conv_bc_weight, conv_bc_bias,
    dt_bias, a_log, norm_gain, reward_w, step_ends,
):
    rows = x_in.shape[0]
    place = lax.axis_index("seq")
    core = place.reshape(1)
    bc = bc_in.reshape(rows, -1)
    tails = jnp.concatenate([x_in[rows - TAIL :], bc_in[rows - TAIL :].reshape(TAIL, -1)], axis=1)
    tails = over(tails, lambda i: i + 1 if i + 1 < 32 else None)
    run, row, ehl, whl, eabs, wabs, tot = decays(dt_in.T, dt_bias[None], a_log[None])
    heads = dt_in.shape[1]
    groups = heads // PER_GROUP
    head = np.arange(heads * HEAD_DIM).reshape(groups, 1, LANES) // HEAD_DIM
    spread = jnp.asarray(np.arange(2 * heads)[:, None] % heads == head, BF16)
    wx, ox = conv_x_weight, conv_x_bias[None]
    made = [[], []]
    for half in range(HALVES):
        for turn in range(2):
            made[turn].append(
                local_states(
                    turn, half, core, x_in, tails, wx, ox, wabs, spread, tot, bc, conv_bc_weight, conv_bc_bias,
                    made[turn][0][0] if half else None,
                )
            )
    values = [None, None]

    def inner(turn, sent):
        m = made[turn]
        values[turn], done = local_values(
            turn, 0, core, m[0][-2], m[0][0], m[0][1], run, row, ehl, whl, spread, sent
        )
        return done[0]

    steps = entering_state(made[0][0][-1], made[1][0][-1])
    sent = next(steps)
    sent = steps.send(inner(1, sent))
    entered = steps.send(inner(0, sent))
    gain, reward, ends = norm_gain[None], reward_w[None], step_ends[None]
    devices = lax.axis_size("seq") * lax.axis_size("head")
    normed, terms = gated_norm(
        1, core, values[1], made[1][0][1], entered[1], eabs, spread, z_in, gain, reward, ends
    )
    normed, terms = gated_norm(
        0, core, values[0], made[0][0][1], entered[0], eabs, spread, z_in, gain, reward, ends,
        (terms, normed), devices,
    )
    terms = lax.all_to_all(terms, ("seq", "head"), 0, 0)
    return normed, jnp.sum(terms, axis=0)


def solution(mesh):
    return jax.shard_map(
        per_device,
        mesh=mesh,
        in_specs=(
            P("seq", "head"),
            P("seq", "head"),
            P("seq", None, "head"),
            P("seq", "head"),
            P(None, "head"),
            P("head"),
            P(None, None, "head"),
            P(None, "head"),
            P("head"),
            P("head"),
            P("head"),
            P("head"),
            P(),
        ),
        out_specs=(P("seq", "head"), P()),
        check_vma=False,
    )
```

```python
import functools

import jax
import jax.numpy as jnp
import numpy as np
from jax import lax
from jax.experimental import pallas as pl
from jax.experimental.pallas import tpu as pltpu
from jax.sharding import PartitionSpec as P

HEAD_DIM = 64
STATE = 256
PER_GROUP = 32
LANES = PER_GROUP * HEAD_DIM
CHUNK = 128
TAIL = 16
EXTRA = 16
TILE = 512
ROWS = 256
BLOCK = 2 * CHUNK
VTILE = 512
HALVES = 1
LOG2E = 1.4426950408889634
F32 = jnp.float32
BF16 = jnp.bfloat16
VMEM_LIMIT = 56 * 1024 * 1024
LESS_VMEM = 24 * 1024 * 1024


def params(*semantics, limit=VMEM_LIMIT):
    return pltpu.CompilerParams(dimension_semantics=semantics or None, vmem_limit_bytes=limit)


def dot(a, b, ca=1, cb=0):
    return lax.dot_general(a, b, (((ca,), (cb,)), ((), ())), preferred_element_type=F32)


def split2(v):
    high = v.astype(BF16)
    return high, (v - high.astype(F32)).astype(BF16)


def split3(v):
    high = v.astype(BF16)
    rest = v - high.astype(F32)
    mid = rest.astype(BF16)
    return high, mid, (rest - mid.astype(F32)).astype(BF16)


def silu_of_twice(half):
    return half + half * jnp.tanh(half)


def silu(v):
    return silu_of_twice(0.5 * v)


def decay_kernel(
    dtin_ref, bias_ref, alog_ref, run_ref, row_ref, ehl_ref, whl_ref, eabs_ref, wabs_ref, tot_ref
):
    heads, rows = dtin_ref.shape
    count = rows // CHUNK
    h0 = lax.broadcasted_iota(jnp.int32, (heads, heads), 0)
    h1 = lax.broadcasted_iota(jnp.int32, (heads, heads), 1)
    upright = lambda v: jnp.sum(jnp.where(h0 == h1, v, 0.0), axis=1, keepdims=True)
    bias = upright(bias_ref[...])
    rate = upright(-LOG2E * jnp.exp(alog_ref[...]))
    u = lax.broadcasted_iota(jnp.int32, (CHUNK, CHUNK), 0)
    t = lax.broadcasted_iota(jnp.int32, (CHUNK, CHUNK), 1)
    upto = (u <= t).astype(BF16)
    after = (u > t).astype(BF16)
    steps, running, suffix, kept = [], [], [], []
    for c in range(count):
        v = dtin_ref[:, c * CHUNK : (c + 1) * CHUNK] + bias
        dt = jnp.maximum(v, 0.0) + jnp.log1p(jnp.exp(-jnp.abs(v)))
        terms = jnp.concatenate(split3(dt * rate), axis=0)
        r = dot(terms, upto)
        s = dot(terms, after)
        r = r[:heads] + r[heads : 2 * heads] + r[2 * heads :]
        s = s[:heads] + s[heads : 2 * heads] + s[2 * heads :]
        steps.append(dt)
        running.append(r)
        suffix.append(s)
    def put(ref, v, c):
        where = slice(c * CHUNK, (c + 1) * CHUNK)
        ref[where, 0:heads], ref[where, heads : 2 * heads] = split2(v)

    whole = jnp.zeros((1, heads), F32)
    for c in range(count):
        where = slice(c * CHUNK, (c + 1) * CHUNK)
        run_ref[:, where] = running[c]
        row_ref[:, where] = running[c] - jnp.log2(steps[c])
        run, rest, dt = running[c].T, suffix[c].T, steps[c].T
        grown, weight = jnp.exp2(run), jnp.exp2(rest) * dt
        put(ehl_ref, grown, c)
        put(whl_ref, weight, c)
        put(eabs_ref, grown * jnp.exp2(whole), c)
        whole = whole + run[CHUNK - 1 :, :]
        kept.append((weight, run[CHUNK - 1 :, :]))
    later = jnp.zeros((1, heads), F32)
    for c in range(count - 1, -1, -1):
        put(wabs_ref, kept[c][0] * jnp.exp2(later), c)
        later = later + kept[c][1]
    high, mid, low = split3(whole)
    place = lax.broadcasted_iota(jnp.int32, (EXTRA, heads), 0)
    terms = jnp.where(
        place == 0,
        high.astype(F32),
        jnp.where(place == 1, mid.astype(F32), jnp.where(place == 2, low.astype(F32), 0.0)),
    ).astype(BF16)
    tot_ref[:, 0:heads] = terms
    tot_ref[:, heads : 2 * heads] = jnp.zeros_like(terms)


def decays(dt_in, bias, a_log):
    heads, rows = dt_in.shape
    pair = jax.ShapeDtypeStruct((rows, 2 * heads), BF16)
    return pl.pallas_call(
        decay_kernel,
        out_shape=[
            jax.ShapeDtypeStruct((heads, rows), F32),
            jax.ShapeDtypeStruct((heads, rows), F32),
            pair,
            pair,
            pair,
            pair,
            jax.ShapeDtypeStruct((EXTRA, 2 * heads), BF16),
        ],
        compiler_params=params(),
        cost_estimate=pl.CostEstimate(flops=10**8, bytes_accessed=2 * 10**6, transcendentals=heads * rows * 5),
    )(dt_in, bias, a_log)


def load_column(pad, series, tail):
    pad[0:8, :] = tail[...].astype(F32)[TAIL - 8 :]
    pad[8 : 8 + series.shape[0], :] = series[...].astype(F32)


def conv_rows(pad, start, taps, offset):
    total = offset + taps[3] * pad[8 + start : 8 + start + CHUNK, :]
    for k in range(3):
        total = total + taps[k] * pad[5 + k + start : 5 + k + start + CHUNK, :]
    return silu_of_twice(total).astype(BF16)


def state_kernel(core_ref, x_ref, xt_ref, wx_ref, ox_ref, wabs_ref, spread_ref, tot_ref, *rest):
    rows = x_ref.shape[0]
    cx_ref, state_ref, pad, scaled, bturn = rest[-5:]
    if len(rest) == 6:
        made_ref = rest[0]

        @pl.when(pl.program_id(0) == 0)
        def _():
            bturn[...] = made_ref[...].T

    else:
        b_ref, bt_ref, c_ref, ct_ref, wb_ref, ob_ref, cb_ref, cc_ref = rest[:8]

        @pl.when(pl.program_id(0) == 0)
        def _():
            for n, (src, tail, dst) in enumerate(((b_ref, bt_ref, cb_ref), (c_ref, ct_ref, cc_ref))):
                for lane in range(0, STATE, 128):
                    own = slice(lane, lane + 128)
                    load_column(pad.at[0], src.at[:, own], tail.at[:, own])
                    taps = [0.5 * wb_ref[k, n : n + 1, own] for k in range(4)]
                    offset = 0.5 * ob_ref[n : n + 1, own]
                    for start in range(0, rows, CHUNK):
                        dst[start : start + CHUNK, own] = conv_rows(pad.at[0], start, taps, offset)
            bturn[...] = cb_ref[...].T

    for lane in range(0, TILE, 256):
        sides = [slice(lane + 128 * n, lane + 128 * n + 128) for n in range(2)]
        for n, own in enumerate(sides):
            load_column(pad.at[n], x_ref.at[:, own], xt_ref.at[:, own])
        taps = [[0.5 * wx_ref[k : k + 1, own] for k in range(4)] for own in sides]
        offsets = [0.5 * ox_ref[:, own] for own in sides]
        for start in range(0, rows, CHUNK):
            here = slice(start, start + CHUNK)
            w = dot(wabs_ref[here, :], spread_ref[0, :, lane : lane + 256])
            for n, own in enumerate(sides):
                v = conv_rows(pad.at[n], start, taps[n], offsets[n])
                cx_ref[here, own] = v
                scaled[here, own] = (w[:, 128 * n : 128 * n + 128] * v.astype(F32)).astype(BF16)
    state_ref[0:STATE, :] = dot(bturn[...], scaled[...]).astype(BF16)
    state_ref[STATE:, :] = dot(tot_ref[...], spread_ref[0]).astype(BF16)


def group_of(turn, core):
    own = lax.rem(core[0], 2)
    return own if turn else 1 - own


def local_states(turn, half, core, x, tails, wx, ox, wabs, spread, tot, bc, wbc, obc, made=None):
    rows, channels = x.shape
    groups = channels // LANES
    width = LANES // HALVES
    tiles = width // TILE
    first = channels // STATE
    lane = lambda j, core: (0, (group_of(turn, core) * HALVES + half) * tiles + j)
    own = lambda shift: lambda j, core: (0, shift + group_of(turn, core))
    still = lambda j, core: (0, 0)
    out = lambda j, core: (0, j)
    if made is None:
        ends = [
            pl.BlockSpec((rows, STATE), own(0)),
            pl.BlockSpec((TAIL, STATE), own(first)),
            pl.BlockSpec((rows, STATE), own(groups)),
            pl.BlockSpec((TAIL, STATE), own(first + groups)),
            pl.BlockSpec((4, 2, STATE), lambda j, core: (0, 0, group_of(turn, core))),
            pl.BlockSpec((2, STATE), own(0)),
        ]
        last = (bc, tails, bc, tails, wbc, obc)
    else:
        ends = [pl.BlockSpec((rows, STATE), still)]
        last = (made,)
    fresh = 2 if made is None else 0
    return pl.pallas_call(
        state_kernel,
        grid_spec=pltpu.PrefetchScalarGridSpec(
            num_scalar_prefetch=1,
            grid=(tiles,),
            in_specs=[
                pl.BlockSpec((rows, TILE), lane),
                pl.BlockSpec((TAIL, TILE), lane),
                pl.BlockSpec((4, TILE), lane),
                pl.BlockSpec((1, TILE), lane),
                pl.BlockSpec(wabs.shape, still),
                pl.BlockSpec((1, spread.shape[1], TILE), lambda j, core: (group_of(turn, core), 0, half * tiles + j)),
                pl.BlockSpec(tot.shape, still),
                *ends,
            ],
            out_specs=[pl.BlockSpec((rows, STATE), still)] * fresh
            + [pl.BlockSpec((rows, TILE), out), pl.BlockSpec((STATE + EXTRA, TILE), out)],
            scratch_shapes=[
                pltpu.VMEM((2, rows + 8, 128), F32),
                pltpu.VMEM((rows, TILE), BF16),
                pltpu.VMEM((STATE, rows), BF16),
            ],
        ),
        out_shape=[jax.ShapeDtypeStruct((rows, STATE), BF16)] * fresh
        + [
            jax.ShapeDtypeStruct((rows, width), BF16),
            jax.ShapeDtypeStruct((STATE + EXTRA, width), BF16),
        ],
        compiler_params=params("arbitrary"),
        cost_estimate=pl.CostEstimate(
            flops=2 * rows * STATE * width, bytes_accessed=4 * rows * width, transcendentals=rows * width
        ),
    )(core, x, tails, wx, ox, wabs, spread, tot, *last)


def values_kernel(
    core_ref, x_ref, b_ref, c_ref, run_ref, row_ref, ehl_ref, whl_ref, spread_ref, sent_ref, out_ref, done_ref, near, inside, across
):
    done_ref[0] = 0
    rows = x_ref.shape[0]
    blocks = rows // BLOCK
    part = lambda n: slice(n * CHUNK, (n + 1) * CHUNK)
    whole = lambda n: slice(n * BLOCK, (n + 1) * BLOCK)
    pairs = [(late, early) for late in range(blocks) for early in range(late)]

    @pl.when(pl.program_id(0) == 0)
    def _():
        t = lax.broadcasted_iota(jnp.int32, (CHUNK, CHUNK), 0)
        s = lax.broadcasted_iota(jnp.int32, (CHUNK, CHUNK), 1)
        for n in range(2 * blocks):
            near[n] = jnp.where(t >= s, dot(c_ref[part(n), :], b_ref[part(n), :], 1, 1), 0.0)
        for n in range(blocks):
            inside[n] = dot(c_ref[part(2 * n + 1), :], b_ref[part(2 * n), :], 1, 1).astype(BF16)
        for n, (late, early) in enumerate(pairs):
            across[n] = dot(c_ref[whole(late), :], b_ref[whole(early), :], 1, 1).astype(BF16)

    left = lax.broadcasted_iota(jnp.int32, (CHUNK, 128), 1) < HEAD_DIM
    turned = [run_ref[:, part(n)].T for n in range(2 * blocks)]
    for lane in range(0, VTILE, 256):
        cut = slice(lane, lane + 256)
        spread = spread_ref[0, :, cut]
        sent, faded = [], []
        for n in range(blocks):
            grown = dot(ehl_ref[whole(n), :], spread)
            weight = dot(whl_ref[whole(n), :], spread)
            x = x_ref[whole(n), cut].astype(F32)
            early_fade = grown[CHUNK - 1 : CHUNK, :]
            late_fade = grown[BLOCK - 1 : BLOCK, :]
            scaled = weight * x
            ended = jnp.concatenate([scaled[:CHUNK] * late_fade, scaled[CHUNK:]], axis=0).astype(BF16)
            sent.append(ended)
            faded.append(early_fade * late_fade)
            carried = None
            for early in range(n):
                came = dot(across[pairs.index((n, early))], sent[early])
                carried = came if carried is None else carried * faded[early] + came
            second = dot(inside[n], scaled[:CHUNK].astype(BF16))
            if carried is not None:
                second = second + carried[CHUNK:] * early_fade
            from_before = (None if carried is None else carried[:CHUNK], second)
            for side in range(2):
                m = 2 * n + side
                base = near[m]
                for pair in range(2):
                    first = lane // HEAD_DIM + 2 * pair
                    low = lane + 128 * pair
                    mixes = []
                    for h in (first, first + 1):
                        along = turned[m][:, h : h + 1] - row_ref[h : h + 1, part(m)]
                        mixes.append((base * jnp.exp2(jnp.minimum(along, 64.0))).astype(BF16))
                    xs = x_ref[part(m), low : low + 128]
                    none = jnp.zeros_like(xs)
                    sides = jnp.concatenate([jnp.where(left, xs, none), jnp.where(left, none, xs)], axis=0)
                    total = dot(jnp.concatenate(mixes, axis=1), sides)
                    if from_before[side] is not None:
                        own = slice(128 * pair, 128 * pair + 128)
                        total = total + grown[side * CHUNK : (side + 1) * CHUNK, own] * from_before[side][:, own]
                    out_ref[part(m), low : low + 128] = total.astype(out_ref.dtype)


def local_values(turn, half, core, x, b, c, run, row, ehl, whl, spread, sent):
    rows, width = x.shape
    blocks = rows // BLOCK
    tiles = width // VTILE
    heads = VTILE // HEAD_DIM
    head = lambda j, core: ((group_of(turn, core) * HALVES + half) * tiles + j, 0)
    still = lambda j, core: (0, 0)
    lane = lambda j, core: (0, j)
    return pl.pallas_call(
        values_kernel,
        grid_spec=pltpu.PrefetchScalarGridSpec(
            num_scalar_prefetch=1,
            grid=(tiles,),
            in_specs=[
                pl.BlockSpec((rows, VTILE), lane),
                pl.BlockSpec((rows, STATE), still),
                pl.BlockSpec((rows, STATE), still),
                pl.BlockSpec((heads, rows), head),
                pl.BlockSpec((heads, rows), head),
                pl.BlockSpec(ehl.shape, still),
                pl.BlockSpec(whl.shape, still),
                pl.BlockSpec((1, spread.shape[1], VTILE), lambda j, core: (group_of(turn, core), 0, half * tiles + j)),
                pl.BlockSpec(memory_space=pl.ANY),
            ],
            out_specs=[pl.BlockSpec((rows, VTILE), lane), pl.BlockSpec(memory_space=pltpu.SMEM)],
            scratch_shapes=[
                pltpu.VMEM((2 * blocks, CHUNK, CHUNK), F32),
                pltpu.VMEM((blocks, CHUNK, CHUNK), BF16),
                pltpu.VMEM((blocks * (blocks - 1) // 2, BLOCK, BLOCK), BF16),
            ],
        ),
        out_shape=[jax.ShapeDtypeStruct((rows, width), BF16), jax.ShapeDtypeStruct((1,), jnp.int32)],
        compiler_params=params("arbitrary"),
        cost_estimate=pl.CostEstimate(
            flops=8 * rows * STATE * width, bytes_accessed=8 * rows * width, transcendentals=rows * CHUNK * width // HEAD_DIM
        ),
    )(core, x, b, c, run, row, ehl, whl, spread, sent)


def norm_kernel(
    devices, place_ref, c_ref, state_ref, values_ref, z_ref, eabs_ref, spread_ref, gain_ref, reward_ref, ends_ref, *rest
):
    earlier = rest[0] if devices else None
    out_ref, term_ref, gated, sums = rest[-4:]
    rows = c_ref.shape[0]
    step = pl.program_id(0)
    c = c_ref[...]
    decay = eabs_ref[...]
    squares = jnp.zeros((rows, 128), F32)
    for lane in range(0, LANES, 256):
        cut = slice(lane, lane + 256)
        v = values_ref[:, cut].astype(F32) + dot(decay, spread_ref[0, :, cut]) * dot(c, state_ref[:, cut])
        v = v * silu(z_ref[:, cut].astype(F32))
        gated[:, cut] = v
        squares = squares + v[:, :128] * v[:, :128] + v[:, 128:] * v[:, 128:]
    scale = lax.rsqrt(jnp.sum(squares, axis=1, keepdims=True) * (1.0 / LANES) + 1e-05)
    terms = jnp.zeros((rows, 128), F32)
    for lane in range(0, LANES, 128):
        cut = slice(lane, lane + 128)
        v = (gated[:, cut] * scale * gain_ref[:, cut]).astype(BF16)
        out_ref[:, cut] = v
        terms = terms + v.astype(F32) * reward_ref[:, cut]
    if devices:
        first = (place_ref[0] * pl.num_programs(0) + step) * rows
        row = lax.broadcasted_iota(jnp.int32, (rows, ends_ref.shape[1]), 0)
        term = jnp.sum(terms + earlier[...], axis=1, keepdims=True)
        found = jnp.where(row == ends_ref[...] - first, term, 0.0)
        found = jnp.sum(found, axis=0, keepdims=True)

        @pl.when(step == 0)
        def _():
            sums[...] = jnp.zeros_like(sums)

        sums[0:1, :] = sums[0:1, :] + found

        @pl.when(step == pl.num_programs(0) - 1)
        def _():
            term_ref[...] = jnp.broadcast_to(sums[0:1, :], term_ref.shape)

    else:
        term_ref[...] = terms


def gated_norm(turn, core, values, c, state, eabs, spread, z, gain, reward, ends, earlier=None, devices=0):
    rows = c.shape[0]
    count = ends.shape[1]
    own = lambda i, core: (i, group_of(turn, core))
    side = lambda i, core: (0, group_of(turn, core))
    down = lambda i, core: (i, 0)
    still = lambda i, core: (0, 0)
    more = [pl.BlockSpec((ROWS, 128), down), pl.BlockSpec(memory_space=pl.ANY)] if devices else []
    terms = (devices, count) if devices else (rows, 128)
    return pl.pallas_call(
        functools.partial(norm_kernel, devices),
        grid_spec=pltpu.PrefetchScalarGridSpec(
            num_scalar_prefetch=1,
            grid=(rows // ROWS,),
            in_specs=[
                pl.BlockSpec((ROWS, STATE), down),
                pl.BlockSpec((STATE, LANES), still),
                pl.BlockSpec((ROWS, LANES), down),
                pl.BlockSpec((ROWS, LANES), own),
                pl.BlockSpec((ROWS, eabs.shape[1]), down),
                pl.BlockSpec((1, spread.shape[1], LANES), lambda i, core: (group_of(turn, core), 0, 0)),
                pl.BlockSpec((1, LANES), side),
                pl.BlockSpec((1, LANES), side),
                pl.BlockSpec((1, count), still),
            ]
            + more,
            out_specs=[
                pl.BlockSpec((ROWS, LANES), own),
                pl.BlockSpec(terms, still) if devices else pl.BlockSpec((ROWS, 128), down),
            ],
            scratch_shapes=[pltpu.VMEM((ROWS, LANES), F32), pltpu.VMEM((8, count), F32)],
        ),
        out_shape=[jax.ShapeDtypeStruct(z.shape, BF16), jax.ShapeDtypeStruct(terms, F32)],
        input_output_aliases={11: 0} if devices else {},
        compiler_params=params("arbitrary", limit=LESS_VMEM),
        cost_estimate=pl.CostEstimate(
            flops=2 * rows * STATE * LANES, bytes_accessed=6 * rows * LANES, transcendentals=rows * LANES
        ),
    )(core, c, state, values, z, eabs, spread, gain, reward, ends, *(earlier or ()))


def total_of(payload):
    extra = payload[STATE : STATE + 3].astype(F32)
    return extra[0:1] + extra[1:2] + extra[2:3]


def with_total(state, total):
    rows = jnp.concatenate(split3(total), axis=0)
    rows = jnp.pad(rows, ((0, EXTRA - 3), (0, 0)))
    return jnp.concatenate([state.astype(BF16), rows], axis=0)


def advance(state, payload):
    return jnp.exp2(total_of(payload)) * state + payload[:STATE].astype(F32)


def over(value, move):
    count = lax.axis_size("seq")
    return lax.ppermute(value, "seq", [(i, move(i)) for i in range(count) if move(i) is not None])


def along_y(k):
    return lambda i: i // 8 * 8 + (i // 2 + k) % 4 * 2 + i % 2


def entering_state(away, mine):
    place = lax.axis_index("seq")
    core = place % 2
    y = place // 2 % 4
    other = over(away, lambda i: i ^ 1)
    first = jnp.where(core == 0, mine, other)
    second = jnp.where(core == 0, other, mine)
    chip = with_total(
        advance(first[:STATE].astype(F32), second), total_of(first) + total_of(second)
    )
    quarter = chip.shape[1] // 4
    piece = lambda n: lax.dynamic_slice_in_dim(chip, n * quarter, quarter, 1)
    going = [piece((y + k) % 4) for k in range(4)]
    came = jnp.stack([going[0]] + [over(going[k], along_y(k)) for k in (1, 2, 3)])
    y = y + (yield going[3])
    parts = [lax.dynamic_index_in_dim(came, (y - n) % 4, 0, False) for n in range(4)]
    state, total = parts[0][:STATE].astype(F32), total_of(parts[0])
    for n in range(1, 4):
        state, total = advance(state, parts[n]), total + total_of(parts[n])
    row = with_total(state, total)
    near, mid, far = (
        over(row, lambda i, k=k: i + 8 * k if i + 8 * k < 32 else None) for k in (1, 2, 3)
    )
    state = advance(advance(far[:STATE].astype(F32), mid), near)
    entering = []
    for n in range(4):
        entering.append(state.astype(BF16))
        state = advance(state, parts[n])
    entering = jnp.stack(entering)
    going = [lax.dynamic_index_in_dim(entering, (y + k) % 4, 0, False) for k in range(4)]
    back = jnp.stack([going[0]] + [over(going[k], along_y(k)) for k in (1, 2, 3)])
    y = y + (yield going[3])
    chip_in = jnp.concatenate(
        [lax.dynamic_index_in_dim(back, (y - n) % 4, 0, False) for n in range(4)], axis=1
    )
    later = advance(chip_in.astype(F32), first).astype(BF16)
    got = over(jnp.where(core == 0, later, chip_in), lambda i: i ^ 1)
    yield got, jnp.where(core == 0, chip_in, later)


def per_device(
    x_in, z_in, bc_in, dt_in, conv_x_weight, conv_x_bias, conv_bc_weight, conv_bc_bias,
    dt_bias, a_log, norm_gain, reward_w, step_ends,
):
    rows = x_in.shape[0]
    place = lax.axis_index("seq")
    core = place.reshape(1)
    bc = bc_in.reshape(rows, -1)
    tails = jnp.concatenate([x_in[rows - TAIL :], bc_in[rows - TAIL :].reshape(TAIL, -1)], axis=1)
    tails = over(tails, lambda i: i + 1 if i + 1 < 32 else None)
    run, row, ehl, whl, eabs, wabs, tot = decays(dt_in.T, dt_bias[None], a_log[None])
    heads = dt_in.shape[1]
    groups = heads // PER_GROUP
    head = np.arange(heads * HEAD_DIM).reshape(groups, 1, LANES) // HEAD_DIM
    spread = jnp.asarray(np.arange(2 * heads)[:, None] % heads == head, BF16)
    wx, ox = conv_x_weight, conv_x_bias[None]
    made = [[], []]
    for half in range(HALVES):
        for turn in range(2):
            made[turn].append(
                local_states(
                    turn, half, core, x_in, tails, wx, ox, wabs, spread, tot, bc, conv_bc_weight, conv_bc_bias,
                    made[turn][0][0] if half else None,
                )
            )
    values = [None, None]

    def inner(turn, sent):
        m = made[turn]
        values[turn], done = local_values(
            turn, 0, core, m[0][-2], m[0][0], m[0][1], run, row, ehl, whl, spread, sent
        )
        return done[0]

    steps = entering_state(made[0][0][-1], made[1][0][-1])
    sent = next(steps)
    sent = steps.send(inner(1, sent))
    entered = steps.send(inner(0, sent))
    gain, reward, ends = norm_gain[None], reward_w[None], step_ends[None]
    devices = lax.axis_size("seq") * lax.axis_size("head")
    normed, terms = gated_norm(
        1, core, values[1], made[1][0][1], entered[1], eabs, spread, z_in, gain, reward, ends
    )
    normed, terms = gated_norm(
        0, core, values[0], made[0][0][1], entered[0], eabs, spread, z_in, gain, reward, ends,
        (terms, normed), devices,
    )
    terms = lax.all_to_all(terms, ("seq", "head"), 0, 0)
    return normed, jnp.sum(terms, axis=0)


def solution(mesh):
    return jax.shard_map(
        per_device,
        mesh=mesh,
        in_specs=(
            P("seq", "head"),
            P("seq", "head"),
            P("seq", None, "head"),
            P("seq", "head"),
            P(None, "head"),
            P("head"),
            P(None, None, "head"),
            P(None, "head"),
            P("head"),
            P("head"),
            P("head"),
            P("head"),
            P(),
        ),
        out_specs=(P("seq", "head"), P()),
        check_vma=False,
    )
```

```python
import functools

import jax
import jax.numpy as jnp
import numpy as np
from jax import lax
from jax.experimental import pallas as pl
from jax.experimental.pallas import tpu as pltpu
from jax.sharding import PartitionSpec as P

HEAD_DIM = 64
STATE = 256
PER_GROUP = 32
LANES = PER_GROUP * HEAD_DIM
CHUNK = 128
TAIL = 16
EXTRA = 16
TILE = 512
ROWS = 256
BLOCK = 2 * CHUNK
VTILE = 512
HALVES = 1
LOG2E = 1.4426950408889634
F32 = jnp.float32
BF16 = jnp.bfloat16
VMEM_LIMIT = 56 * 1024 * 1024
LESS_VMEM = 24 * 1024 * 1024


def params(*semantics, limit=VMEM_LIMIT):
    return pltpu.CompilerParams(dimension_semantics=semantics or None, vmem_limit_bytes=limit)


def dot(a, b, ca=1, cb=0):
    return lax.dot_general(a, b, (((ca,), (cb,)), ((), ())), preferred_element_type=F32)


def split2(v):
    high = v.astype(BF16)
    return high, (v - high.astype(F32)).astype(BF16)


def split3(v):
    high = v.astype(BF16)
    rest = v - high.astype(F32)
    mid = rest.astype(BF16)
    return high, mid, (rest - mid.astype(F32)).astype(BF16)


def silu_of_twice(half):
    return half + half * jnp.tanh(half)


def silu(v):
    return silu_of_twice(0.5 * v)


def decay_kernel(
    dtin_ref, bias_ref, alog_ref, run_ref, row_ref, ehl_ref, whl_ref, eabs_ref, wabs_ref, tot_ref
):
    heads, rows = dtin_ref.shape
    count = rows // CHUNK
    h0 = lax.broadcasted_iota(jnp.int32, (heads, heads), 0)
    h1 = lax.broadcasted_iota(jnp.int32, (heads, heads), 1)
    upright = lambda v: jnp.sum(jnp.where(h0 == h1, v, 0.0), axis=1, keepdims=True)
    bias = upright(bias_ref[...])
    rate = upright(-LOG2E * jnp.exp(alog_ref[...]))
    u = lax.broadcasted_iota(jnp.int32, (CHUNK, CHUNK), 0)
    t = lax.broadcasted_iota(jnp.int32, (CHUNK, CHUNK), 1)
    upto = (u <= t).astype(BF16)
    after = (u > t).astype(BF16)
    steps, running, suffix, kept = [], [], [], []
    for c in range(count):
        v = dtin_ref[:, c * CHUNK : (c + 1) * CHUNK] + bias
        dt = jnp.maximum(v, 0.0) + jnp.log1p(jnp.exp(-jnp.abs(v)))
        terms = jnp.concatenate(split3(dt * rate), axis=0)
        r = dot(terms, upto)
        s = dot(terms, after)
        r = r[:heads] + r[heads : 2 * heads] + r[2 * heads :]
        s = s[:heads] + s[heads : 2 * heads] + s[2 * heads :]
        steps.append(dt)
        running.append(r)
        suffix.append(s)
    def put(ref, v, c):
        where = slice(c * CHUNK, (c + 1) * CHUNK)
        ref[where, 0:heads], ref[where, heads : 2 * heads] = split2(v)

    whole = jnp.zeros((1, heads), F32)
    for c in range(count):
        where = slice(c * CHUNK, (c + 1) * CHUNK)
        run_ref[:, where] = running[c]
        row_ref[:, where] = running[c] - jnp.log2(steps[c])
        run, rest, dt = running[c].T, suffix[c].T, steps[c].T
        grown, weight = jnp.exp2(run), jnp.exp2(rest) * dt
        put(ehl_ref, grown, c)
        put(whl_ref, weight, c)
        put(eabs_ref, grown * jnp.exp2(whole), c)
        whole = whole + run[CHUNK - 1 :, :]
        kept.append((weight, run[CHUNK - 1 :, :]))
    later = jnp.zeros((1, heads), F32)
    for c in range(count - 1, -1, -1):
        put(wabs_ref, kept[c][0] * jnp.exp2(later), c)
        later = later + kept[c][1]
    high, mid, low = split3(whole)
    place = lax.broadcasted_iota(jnp.int32, (EXTRA, heads), 0)
    terms = jnp.where(
        place == 0,
        high.astype(F32),
        jnp.where(place == 1, mid.astype(F32), jnp.where(place == 2, low.astype(F32), 0.0)),
    ).astype(BF16)
    tot_ref[:, 0:heads] = terms
    tot_ref[:, heads : 2 * heads] = jnp.zeros_like(terms)


def decays(dt_in, bias, a_log):
    heads, rows = dt_in.shape
    pair = jax.ShapeDtypeStruct((rows, 2 * heads), BF16)
    return pl.pallas_call(
        decay_kernel,
        out_shape=[
            jax.ShapeDtypeStruct((heads, rows), F32),
            jax.ShapeDtypeStruct((heads, rows), F32),
            pair,
            pair,
            pair,
            pair,
            jax.ShapeDtypeStruct((EXTRA, 2 * heads), BF16),
        ],
        compiler_params=params(),
        cost_estimate=pl.CostEstimate(flops=10**8, bytes_accessed=2 * 10**6, transcendentals=heads * rows * 5),
    )(dt_in, bias, a_log)


def load_column(pad, series, tail):
    pad[0:8, :] = tail[...].astype(F32)[TAIL - 8 :]
    pad[8 : 8 + series.shape[0], :] = series[...].astype(F32)


def conv_rows(pad, start, taps, offset):
    total = offset + taps[3] * pad[8 + start : 8 + start + CHUNK, :]
    for k in range(3):
        total = total + taps[k] * pad[5 + k + start : 5 + k + start + CHUNK, :]
    return silu_of_twice(total).astype(BF16)


def conv_state(pad, src, tail, taps_ref, offset_ref, n, dst):
    for lane in range(0, STATE, 128):
        own = slice(lane, lane + 128)
        load_column(pad, src.at[:, own], tail.at[:, own])
        taps = [0.5 * taps_ref[k, n : n + 1, own] for k in range(4)]
        offset = 0.5 * offset_ref[n : n + 1, own]
        for start in range(0, src.shape[0], CHUNK):
            dst[start : start + CHUNK, own] = conv_rows(pad, start, taps, offset)


def state_kernel(core_ref, x_ref, xt_ref, wx_ref, ox_ref, wabs_ref, spread_ref, tot_ref, *rest):
    rows = x_ref.shape[0]
    cx_ref, state_ref, pad, scaled, bturn = rest[-5:]
    if len(rest) == 6:
        made_ref = rest[0]

        @pl.when(pl.program_id(0) == 0)
        def _():
            bturn[...] = made_ref[...].T

    else:
        b_ref, bt_ref, wb_ref, ob_ref, cb_ref = rest[:5]

        @pl.when(pl.program_id(0) == 0)
        def _():
            conv_state(pad.at[0], b_ref, bt_ref, wb_ref, ob_ref, 0, cb_ref)
            bturn[...] = cb_ref[...].T

    for lane in range(0, TILE, 256):
        sides = [slice(lane + 128 * n, lane + 128 * n + 128) for n in range(2)]
        for n, own in enumerate(sides):
            load_column(pad.at[n], x_ref.at[:, own], xt_ref.at[:, own])
        taps = [[0.5 * wx_ref[k : k + 1, own] for k in range(4)] for own in sides]
        offsets = [0.5 * ox_ref[:, own] for own in sides]
        for start in range(0, rows, CHUNK):
            here = slice(start, start + CHUNK)
            w = dot(wabs_ref[here, :], spread_ref[0, :, lane : lane + 256])
            for n, own in enumerate(sides):
                v = conv_rows(pad.at[n], start, taps[n], offsets[n])
                cx_ref[here, own] = v
                scaled[here, own] = (w[:, 128 * n : 128 * n + 128] * v.astype(F32)).astype(BF16)
    state_ref[0:STATE, :] = dot(bturn[...], scaled[...]).astype(BF16)
    state_ref[STATE:, :] = dot(tot_ref[...], spread_ref[0]).astype(BF16)


def group_of(turn, core):
    own = lax.rem(core[0], 2)
    return own if turn else 1 - own


def local_states(turn, half, core, x, tails, wx, ox, wabs, spread, tot, bc, wbc, obc, made=None):
    rows, channels = x.shape
    groups = channels // LANES
    width = LANES // HALVES
    tiles = width // TILE
    first = channels // STATE
    lane = lambda j, core: (0, (group_of(turn, core) * HALVES + half) * tiles + j)
    own = lambda shift: lambda j, core: (0, shift + group_of(turn, core))
    still = lambda j, core: (0, 0)
    out = lambda j, core: (0, j)
    if made is None:
        ends = [
            pl.BlockSpec((rows, STATE), own(0)),
            pl.BlockSpec((TAIL, STATE), own(first)),
            pl.BlockSpec((4, 2, STATE), lambda j, core: (0, 0, group_of(turn, core))),
            pl.BlockSpec((2, STATE), own(0)),
        ]
        last = (bc, tails, wbc, obc)
    else:
        ends = [pl.BlockSpec((rows, STATE), still)]
        last = (made,)
    fresh = 1 if made is None else 0
    return pl.pallas_call(
        state_kernel,
        grid_spec=pltpu.PrefetchScalarGridSpec(
            num_scalar_prefetch=1,
            grid=(tiles,),
            in_specs=[
                pl.BlockSpec((rows, TILE), lane),
                pl.BlockSpec((TAIL, TILE), lane),
                pl.BlockSpec((4, TILE), lane),
                pl.BlockSpec((1, TILE), lane),
                pl.BlockSpec(wabs.shape, still),
                pl.BlockSpec((1, spread.shape[1], TILE), lambda j, core: (group_of(turn, core), 0, half * tiles + j)),
                pl.BlockSpec(tot.shape, still),
                *ends,
            ],
            out_specs=[pl.BlockSpec((rows, STATE), still)] * fresh
            + [pl.BlockSpec((rows, TILE), out), pl.BlockSpec((STATE + EXTRA, TILE), out)],
            scratch_shapes=[
                pltpu.VMEM((2, rows + 8, 128), F32),
                pltpu.VMEM((rows, TILE), BF16),
                pltpu.VMEM((STATE, rows), BF16),
            ],
        ),
        out_shape=[jax.ShapeDtypeStruct((rows, STATE), BF16)] * fresh
        + [
            jax.ShapeDtypeStruct((rows, width), BF16),
            jax.ShapeDtypeStruct((STATE + EXTRA, width), BF16),
        ],
        compiler_params=params("arbitrary"),
        cost_estimate=pl.CostEstimate(
            flops=2 * rows * STATE * width, bytes_accessed=4 * rows * width, transcendentals=rows * width
        ),
    )(core, x, tails, wx, ox, wabs, spread, tot, *last)


def values_kernel(
    core_ref, x_ref, b_ref, ci_ref, ct_ref, wb_ref, ob_ref, run_ref, row_ref, ehl_ref, whl_ref, spread_ref, sent_ref,
    out_ref, c_ref, done_ref, pad, near, inside, across,
):
    done_ref[0] = 0
    rows = x_ref.shape[0]
    blocks = rows // BLOCK
    part = lambda n: slice(n * CHUNK, (n + 1) * CHUNK)
    whole = lambda n: slice(n * BLOCK, (n + 1) * BLOCK)
    pairs = [(late, early) for late in range(blocks) for early in range(late)]

    @pl.when(pl.program_id(0) == 0)
    def _():
        conv_state(pad, ci_ref, ct_ref, wb_ref, ob_ref, 1, c_ref)
        t = lax.broadcasted_iota(jnp.int32, (CHUNK, CHUNK), 0)
        s = lax.broadcasted_iota(jnp.int32, (CHUNK, CHUNK), 1)
        for n in range(2 * blocks):
            near[n] = jnp.where(t >= s, dot(c_ref[part(n), :], b_ref[part(n), :], 1, 1), 0.0)
        for n in range(blocks):
            inside[n] = dot(c_ref[part(2 * n + 1), :], b_ref[part(2 * n), :], 1, 1).astype(BF16)
        for n, (late, early) in enumerate(pairs):
            across[n] = dot(c_ref[whole(late), :], b_ref[whole(early), :], 1, 1).astype(BF16)

    left = lax.broadcasted_iota(jnp.int32, (CHUNK, 128), 1) < HEAD_DIM
    turned = [run_ref[:, part(n)].T for n in range(2 * blocks)]
    for lane in range(0, VTILE, 256):
        cut = slice(lane, lane + 256)
        spread = spread_ref[0, :, cut]
        sent, faded = [], []
        for n in range(blocks):
            grown = dot(ehl_ref[whole(n), :], spread)
            weight = dot(whl_ref[whole(n), :], spread)
            x = x_ref[whole(n), cut].astype(F32)
            early_fade = grown[CHUNK - 1 : CHUNK, :]
            late_fade = grown[BLOCK - 1 : BLOCK, :]
            scaled = weight * x
            ended = jnp.concatenate([scaled[:CHUNK] * late_fade, scaled[CHUNK:]], axis=0).astype(BF16)
            sent.append(ended)
            faded.append(early_fade * late_fade)
            carried = None
            for early in range(n):
                came = dot(across[pairs.index((n, early))], sent[early])
                carried = came if carried is None else carried * faded[early] + came
            second = dot(inside[n], scaled[:CHUNK].astype(BF16))
            if carried is not None:
                second = second + carried[CHUNK:] * early_fade
            from_before = (None if carried is None else carried[:CHUNK], second)
            for side in range(2):
                m = 2 * n + side
                base = near[m]
                for pair in range(2):
                    first = lane // HEAD_DIM + 2 * pair
                    low = lane + 128 * pair
                    mixes = []
                    for h in (first, first + 1):
                        along = turned[m][:, h : h + 1] - row_ref[h : h + 1, part(m)]
                        mixes.append((base * jnp.exp2(jnp.minimum(along, 64.0))).astype(BF16))
                    xs = x_ref[part(m), low : low + 128]
                    none = jnp.zeros_like(xs)
                    sides = jnp.concatenate([jnp.where(left, xs, none), jnp.where(left, none, xs)], axis=0)
                    total = dot(jnp.concatenate(mixes, axis=1), sides)
                    if from_before[side] is not None:
                        own = slice(128 * pair, 128 * pair + 128)
                        total = total + grown[side * CHUNK : (side + 1) * CHUNK, own] * from_before[side][:, own]
                    out_ref[part(m), low : low + 128] = total.astype(out_ref.dtype)


def local_values(turn, half, core, x, b, bc, tails, wbc, obc, run, row, ehl, whl, spread, sent):
    rows, width = x.shape
    groups = bc.shape[1] // (2 * STATE)
    first = tails.shape[1] // STATE - groups
    own = lambda shift: lambda j, core: (0, shift + group_of(turn, core))
    blocks = rows // BLOCK
    tiles = width // VTILE
    heads = VTILE // HEAD_DIM
    head = lambda j, core: ((group_of(turn, core) * HALVES + half) * tiles + j, 0)
    still = lambda j, core: (0, 0)
    lane = lambda j, core: (0, j)
    return pl.pallas_call(
        values_kernel,
        grid_spec=pltpu.PrefetchScalarGridSpec(
            num_scalar_prefetch=1,
            grid=(tiles,),
            in_specs=[
                pl.BlockSpec((rows, VTILE), lane),
                pl.BlockSpec((rows, STATE), still),
                pl.BlockSpec((rows, STATE), own(groups)),
                pl.BlockSpec((TAIL, STATE), own(first)),
                pl.BlockSpec((4, 2, STATE), lambda j, core: (0, 0, group_of(turn, core))),
                pl.BlockSpec((2, STATE), own(0)),
                pl.BlockSpec((heads, rows), head),
                pl.BlockSpec((heads, rows), head),
                pl.BlockSpec(ehl.shape, still),
                pl.BlockSpec(whl.shape, still),
                pl.BlockSpec((1, spread.shape[1], VTILE), lambda j, core: (group_of(turn, core), 0, half * tiles + j)),
                pl.BlockSpec(memory_space=pl.ANY),
            ],
            out_specs=[
                pl.BlockSpec((rows, VTILE), lane),
                pl.BlockSpec((rows, STATE), still),
                pl.BlockSpec(memory_space=pltpu.SMEM),
            ],
            scratch_shapes=[
                pltpu.VMEM((rows + 8, 128), F32),
                pltpu.VMEM((2 * blocks, CHUNK, CHUNK), F32),
                pltpu.VMEM((blocks, CHUNK, CHUNK), BF16),
                pltpu.VMEM((blocks * (blocks - 1) // 2, BLOCK, BLOCK), BF16),
            ],
        ),
        out_shape=[
            jax.ShapeDtypeStruct((rows, width), BF16),
            jax.ShapeDtypeStruct((rows, STATE), BF16),
            jax.ShapeDtypeStruct((1,), jnp.int32),
        ],
        compiler_params=params("arbitrary"),
        cost_estimate=pl.CostEstimate(
            flops=8 * rows * STATE * width, bytes_accessed=8 * rows * width, transcendentals=rows * CHUNK * width // HEAD_DIM
        ),
    )(core, x, b, bc, tails, wbc, obc, run, row, ehl, whl, spread, sent)


def norm_kernel(
    devices, place_ref, c_ref, state_ref, values_ref, z_ref, eabs_ref, spread_ref, gain_ref, reward_ref, ends_ref, *rest
):
    earlier = rest[0] if devices else None
    out_ref, term_ref, gated, sums = rest[-4:]
    rows = c_ref.shape[0]
    step = pl.program_id(0)
    c = c_ref[...]
    decay = eabs_ref[...]
    squares = jnp.zeros((rows, 128), F32)
    for lane in range(0, LANES, 256):
        cut = slice(lane, lane + 256)
        v = values_ref[:, cut].astype(F32) + dot(decay, spread_ref[0, :, cut]) * dot(c, state_ref[:, cut])
        v = v * silu(z_ref[:, cut].astype(F32))
        gated[:, cut] = v
        squares = squares + v[:, :128] * v[:, :128] + v[:, 128:] * v[:, 128:]
    scale = lax.rsqrt(jnp.sum(squares, axis=1, keepdims=True) * (1.0 / LANES) + 1e-05)
    terms = jnp.zeros((rows, 128), F32)
    for lane in range(0, LANES, 128):
        cut = slice(lane, lane + 128)
        v = (gated[:, cut] * scale * gain_ref[:, cut]).astype(BF16)
        out_ref[:, cut] = v
        terms = terms + v.astype(F32) * reward_ref[:, cut]
    if devices:
        first = (place_ref[0] * pl.num_programs(0) + step) * rows
        row = lax.broadcasted_iota(jnp.int32, (rows, ends_ref.shape[1]), 0)
        term = jnp.sum(terms + earlier[...], axis=1, keepdims=True)
        found = jnp.where(row == ends_ref[...] - first, term, 0.0)
        found = jnp.sum(found, axis=0, keepdims=True)

        @pl.when(step == 0)
        def _():
            sums[...] = jnp.zeros_like(sums)

        sums[0:1, :] = sums[0:1, :] + found

        @pl.when(step == pl.num_programs(0) - 1)
        def _():
            term_ref[...] = jnp.broadcast_to(sums[0:1, :], term_ref.shape)

    else:
        term_ref[...] = terms


def gated_norm(turn, core, values, c, state, eabs, spread, z, gain, reward, ends, earlier=None, devices=0):
    rows = c.shape[0]
    count = ends.shape[1]
    own = lambda i, core: (i, group_of(turn, core))
    side = lambda i, core: (0, group_of(turn, core))
    down = lambda i, core: (i, 0)
    still = lambda i, core: (0, 0)
    more = [pl.BlockSpec((ROWS, 128), down), pl.BlockSpec(memory_space=pl.ANY)] if devices else []
    terms = (devices, count) if devices else (rows, 128)
    return pl.pallas_call(
        functools.partial(norm_kernel, devices),
        grid_spec=pltpu.PrefetchScalarGridSpec(
            num_scalar_prefetch=1,
            grid=(rows // ROWS,),
            in_specs=[
                pl.BlockSpec((ROWS, STATE), down),
                pl.BlockSpec((STATE, LANES), still),
                pl.BlockSpec((ROWS, LANES), down),
                pl.BlockSpec((ROWS, LANES), own),
                pl.BlockSpec((ROWS, eabs.shape[1]), down),
                pl.BlockSpec((1, spread.shape[1], LANES), lambda i, core: (group_of(turn, core), 0, 0)),
                pl.BlockSpec((1, LANES), side),
                pl.BlockSpec((1, LANES), side),
                pl.BlockSpec((1, count), still),
            ]
            + more,
            out_specs=[
                pl.BlockSpec((ROWS, LANES), own),
                pl.BlockSpec(terms, still) if devices else pl.BlockSpec((ROWS, 128), down),
            ],
            scratch_shapes=[pltpu.VMEM((ROWS, LANES), F32), pltpu.VMEM((8, count), F32)],
        ),
        out_shape=[jax.ShapeDtypeStruct(z.shape, BF16), jax.ShapeDtypeStruct(terms, F32)],
        input_output_aliases={11: 0} if devices else {},
        compiler_params=params("arbitrary", limit=LESS_VMEM),
        cost_estimate=pl.CostEstimate(
            flops=2 * rows * STATE * LANES, bytes_accessed=6 * rows * LANES, transcendentals=rows * LANES
        ),
    )(core, c, state, values, z, eabs, spread, gain, reward, ends, *(earlier or ()))


def total_of(payload):
    extra = payload[STATE : STATE + 3].astype(F32)
    return extra[0:1] + extra[1:2] + extra[2:3]


def with_total(state, total):
    rows = jnp.concatenate(split3(total), axis=0)
    rows = jnp.pad(rows, ((0, EXTRA - 3), (0, 0)))
    return jnp.concatenate([state.astype(BF16), rows], axis=0)


def advance(state, payload):
    return jnp.exp2(total_of(payload)) * state + payload[:STATE].astype(F32)


def over(value, move):
    count = lax.axis_size("seq")
    return lax.ppermute(value, "seq", [(i, move(i)) for i in range(count) if move(i) is not None])


def along_y(k):
    return lambda i: i // 8 * 8 + (i // 2 + k) % 4 * 2 + i % 2


def entering_state(away, mine):
    place = lax.axis_index("seq")
    core = place % 2
    y = place // 2 % 4
    other = over(away, lambda i: i ^ 1)
    first = jnp.where(core == 0, mine, other)
    second = jnp.where(core == 0, other, mine)
    chip = with_total(
        advance(first[:STATE].astype(F32), second), total_of(first) + total_of(second)
    )
    quarter = chip.shape[1] // 4
    piece = lambda n: lax.dynamic_slice_in_dim(chip, n * quarter, quarter, 1)
    going = [piece((y + k) % 4) for k in range(4)]
    came = jnp.stack([going[0]] + [over(going[k], along_y(k)) for k in (1, 2, 3)])
    y = y + (yield going[3])
    parts = [lax.dynamic_index_in_dim(came, (y - n) % 4, 0, False) for n in range(4)]
    state, total = parts[0][:STATE].astype(F32), total_of(parts[0])
    for n in range(1, 4):
        state, total = advance(state, parts[n]), total + total_of(parts[n])
    row = with_total(state, total)
    near, mid, far = (
        over(row, lambda i, k=k: i + 8 * k if i + 8 * k < 32 else None) for k in (1, 2, 3)
    )
    state = advance(advance(far[:STATE].astype(F32), mid), near)
    entering = []
    for n in range(4):
        entering.append(state.astype(BF16))
        state = advance(state, parts[n])
    entering = jnp.stack(entering)
    going = [lax.dynamic_index_in_dim(entering, (y + k) % 4, 0, False) for k in range(4)]
    back = jnp.stack([going[0]] + [over(going[k], along_y(k)) for k in (1, 2, 3)])
    y = y + (yield going[3])
    chip_in = jnp.concatenate(
        [lax.dynamic_index_in_dim(back, (y - n) % 4, 0, False) for n in range(4)], axis=1
    )
    later = advance(chip_in.astype(F32), first).astype(BF16)
    got = over(jnp.where(core == 0, later, chip_in), lambda i: i ^ 1)
    yield got, jnp.where(core == 0, chip_in, later)


def per_device(
    x_in, z_in, bc_in, dt_in, conv_x_weight, conv_x_bias, conv_bc_weight, conv_bc_bias,
    dt_bias, a_log, norm_gain, reward_w, step_ends,
):
    rows = x_in.shape[0]
    place = lax.axis_index("seq")
    core = place.reshape(1)
    bc = bc_in.reshape(rows, -1)
    tails = jnp.concatenate([x_in[rows - TAIL :], bc_in[rows - TAIL :].reshape(TAIL, -1)], axis=1)
    tails = over(tails, lambda i: i + 1 if i + 1 < 32 else None)
    run, row, ehl, whl, eabs, wabs, tot = decays(dt_in.T, dt_bias[None], a_log[None])
    heads = dt_in.shape[1]
    groups = heads // PER_GROUP
    head = np.arange(heads * HEAD_DIM).reshape(groups, 1, LANES) // HEAD_DIM
    spread = jnp.asarray(np.arange(2 * heads)[:, None] % heads == head, BF16)
    wx, ox = conv_x_weight, conv_x_bias[None]
    made = [[], []]
    for half in range(HALVES):
        for turn in range(2):
            made[turn].append(
                local_states(
                    turn, half, core, x_in, tails, wx, ox, wabs, spread, tot, bc, conv_bc_weight, conv_bc_bias,
                    made[turn][0][0] if half else None,
                )
            )
    values, outward = [None, None], [None, None]

    def inner(turn, sent):
        m = made[turn][0]
        values[turn], outward[turn], done = local_values(
            turn, 0, core, m[-2], m[0], bc, tails, conv_bc_weight, conv_bc_bias, run, row, ehl, whl, spread, sent
        )
        return done[0]

    steps = entering_state(made[0][0][-1], made[1][0][-1])
    sent = next(steps)
    sent = steps.send(inner(1, sent))
    entered = steps.send(inner(0, sent))
    gain, reward, ends = norm_gain[None], reward_w[None], step_ends[None]
    devices = lax.axis_size("seq") * lax.axis_size("head")
    normed, terms = gated_norm(
        1, core, values[1], outward[1], entered[1], eabs, spread, z_in, gain, reward, ends
    )
    normed, terms = gated_norm(
        0, core, values[0], outward[0], entered[0], eabs, spread, z_in, gain, reward, ends,
        (terms, normed), devices,
    )
    terms = lax.all_to_all(terms, ("seq", "head"), 0, 0)
    return normed, jnp.sum(terms, axis=0)


def solution(mesh):
    return jax.shard_map(
        per_device,
        mesh=mesh,
        in_specs=(
            P("seq", "head"),
            P("seq", "head"),
            P("seq", None, "head"),
            P("seq", "head"),
            P(None, "head"),
            P("head"),
            P(None, None, "head"),
            P(None, "head"),
            P("head"),
            P("head"),
            P("head"),
            P("head"),
            P(),
        ),
        out_specs=(P("seq", "head"), P()),
        check_vma=False,
    )
```
